512 devices in a mesh: dom: 64 (over x, z, core), col: 8 (over y).
Axes of the slice: x: 4, y: 8, z: 8, core: 2. Of those that a mesh axis runs over, the one named last changes fastest.
Arguments:
- feats: bfloat16 [128, 131072], P('col', 'dom'), may hold values from -6 to 6
- part_len: int32 [64], P('dom'), may hold values from 1 to 2048, 98304 in all
- loc_vals: bfloat16 [1536, 128, 128], P('dom'), may hold values from -0.375 to 0.375
- loc_coord: int32 [1536, 2], P('dom'), may hold values from 0 to 15
- send_block: int32 [64, 64], P('dom'), may hold values from 0 to 15
- send_live: int32 [64, 64], P('dom'), may hold values 0 or 1
- rem_vals: bfloat16 [4096, 128, 128], P('dom'), may hold values from -0.375 to 0.375
- rem_dst: int32 [64, 64], P('dom'), may hold values from 0 to 15
- weight: bfloat16 [2, 128, 256], replicated, may hold values from -0.375 to 0.375
- bias: float32 [256], replicated, may hold values from -3 to 3
- cot: bfloat16 [256, 131072], P(None, ('dom', 'col')), may hold values from -6 to 6
Outputs:
- hidden: bfloat16 [256, 131072], P(None, ('dom', 'col'))
- grad_feats: float32 [128, 131072], P('col', 'dom')
- grad_weight: float32 [2, 128, 256], P(None, 'col')
- grad_bias: float32 [256], replicated
The draws below stay inside these ranges and needn't reach their ends.
Inputs may be any that keep to these rules, and one draw needn't show every extreme that they name: `part_len`: one partition holds exactly 2048 live nodes. `loc_coord`: blocks may repeat; repeated blocks add.
All inputs are finite; a program needn't handle non-finite values. No bound on the sum of `part_len` or of `send_live` on one device may be relied on, other than what follows from the above.
Results may differ from the reference program's by a relative error of at most 0.014.
Values may be sent and summed in bfloat16 or wider, within the bound.
No kernel may reach another device: no remote copies, remote signals or barrier semaphores. Data moves between devices by JAX's collectives and lax.ppermute only.
A program may use at most 64 MiB of HBM per device.

```python
import math
import jax
import jax.numpy as jnp
import numpy as np
from jax import lax

F = 128
H = 256
BLK = 128
NODE_DEV = 2048
NB = 16
LOC = 24
NODES = 131072
N_DOM = 64


def plant(values, own_key, least, largest):
    longest = values.shape.index(max(values.shape))
    spots = []
    for shift in (0, 1):
        where = [jax.random.randint(jax.random.fold_in(own_key, axis), (), 0, length) for axis, length in enumerate(values.shape)]
        where[longest] = (where[longest] + shift) % values.shape[longest]
        spots.append(tuple(where))
    return values.at[spots[0]].set(least).at[spots[1]].set(largest)


def block_scale(stream_key, dims, split, least, top_value):
    gain = 1.0
    for dim, blocks in split:
        heights = jax.random.uniform(jax.random.fold_in(jax.random.fold_in(stream_key, 6), dim), (blocks,), jnp.float32, least / len(split), top_value / len(split))
        gain = gain * jnp.repeat(jnp.exp(heights), dims[dim] // blocks).reshape((-1,) + (1,) * (len(dims) - 1 - dim))
    return gain


def profile(amount, total, limit, lean):
    portions = [(1 << 20) // math.isqrt(rank ** lean) + 1 for rank in range(2, amount + 1)]
    surplus, given = total - limit - (amount - 1), [1] * (amount - 1)
    while surplus > 0:
        candidates = [i for i in range(amount - 1) if given[i] < limit]
        whole, left = sum([portions[i] for i in candidates]), surplus
        for i in candidates:
            more = min(limit - given[i], max(1, left * portions[i] // whole), surplus)
            given[i] = given[i] + more
            surplus = surplus - more
    return np.array([limit] + given)


def ragged_sizes(stream_key, number_of, total, reach, lean):
    if number_of == 2:
        one = jax.random.randint(stream_key, (), max(1, total - reach), min(reach, total - 1) + 1)
        return jnp.stack([one, total - one])
    lengths = jnp.asarray(profile(number_of, total, reach, lean), jnp.int32)
    couples = (number_of - 1) // 2
    donor, receiver = lengths[1:1 + 2 * couples:2], lengths[2:2 + 2 * couples:2]
    margin = jnp.minimum(donor - 1, reach - receiver)
    passed = jax.random.randint(jax.random.fold_in(stream_key, 1), (couples,), 0, 1 << 20) % (margin + 1)
    lengths = lengths.at[1:1 + 2 * couples:2].set(donor - passed).at[2:2 + 2 * couples:2].set(receiver + passed)
    return lengths[jax.random.permutation(jax.random.fold_in(stream_key, 2), number_of)]


def scatter_about(stream_key, shape, deviation, most, split=(), kind=jnp.bfloat16):
    entries = deviation * jax.random.normal(stream_key, shape, jnp.float32)
    if split:
        entries = entries * block_scale(stream_key, shape, split, -0.22, 0.18)
    return jnp.clip(entries, -most, most).astype(kind)


def setup_inputs(seed: int = 0) -> dict:
    seeds = jax.random.split(jax.random.key(seed), 12)
    return {
        "feats": scatter_about(seeds[0], (F, NODES), 1.0, 6.0, ((0, 8), (1, 64))),
        "part_len": ragged_sizes(seeds[1], N_DOM, N_DOM * NODE_DEV * 3 // 4, NODE_DEV, 0).astype(jnp.int32),
        "loc_vals": scatter_about(seeds[2], (N_DOM * LOC, BLK, BLK), (BLK * 2) ** -0.5, 0.375, ((0, 64),)),
        "loc_coord": plant(jax.random.randint(seeds[3], (N_DOM * LOC, 2), 0, NB), jax.random.fold_in(seeds[3], 1), 0, NB - 1).astype(jnp.int32),
        "send_block": plant(jax.random.randint(seeds[4], (N_DOM, N_DOM), 0, NB), jax.random.fold_in(seeds[4], 1), 0, NB - 1).astype(jnp.int32),
        "send_live": plant((jax.random.randint(seeds[5], (N_DOM, N_DOM), 0, 2) < 1).astype(jnp.int32), jax.random.fold_in(seeds[5], 1), 0, 1),
        "rem_vals": scatter_about(seeds[6], (N_DOM * N_DOM, BLK, BLK), (BLK * 2) ** -0.5, 0.375, ((0, 64),)),
        "rem_dst": plant(jax.random.randint(seeds[7], (N_DOM, N_DOM), 0, NB), jax.random.fold_in(seeds[7], 1), 0, NB - 1).astype(jnp.int32),
        "weight": scatter_about(seeds[8], (2, F, H), (2 * F) ** -0.5, 0.375),
        "bias": scatter_about(seeds[9], (H,), 0.5, 3.0, (), jnp.float32),
        "cot": scatter_about(seeds[10], (H, NODES), 1.0, 6.0, ((1, 512),)),
    }


def reference(feats, part_len, loc_vals, loc_coord, send_block, send_live, rem_vals, rem_dst, weight, bias, cot):
    f32 = jnp.float32
    nblocks = NODE_DEV // BLK
    node_ids = jnp.arange(NODES, dtype=jnp.int32)
    owner = node_ids // NODE_DEV
    local = node_ids % NODE_DEV
    mask = (local < part_len[owner]).astype(f32)
    xm = jnp.where(mask[None, :] > 0, feats, jnp.zeros_like(feats))
    xblocks = xm.reshape(F, N_DOM, nblocks, BLK).transpose(1, 2, 0, 3)
    lvals = loc_vals.reshape(N_DOM, LOC, BLK, BLK)
    lcoord = loc_coord.reshape(N_DOM, LOC, 2)
    rvals = rem_vals.reshape(N_DOM, N_DOM, BLK, BLK)
    rowids = jnp.arange(nblocks, dtype=jnp.int32)
    parts = jnp.arange(N_DOM, dtype=jnp.int32)
    live = send_live.astype(f32)

    def gather_one(p):
        xpart = xblocks[p]
        lgot = xpart[lcoord[p, :, 0]].astype(f32)
        lterm = jnp.einsum('kfs,ksd->kfd', lgot, lvals[p].astype(f32))
        lsel = (lcoord[p, :, 1][None, :] == rowids[:, None]).astype(f32)
        total = jnp.einsum('rk,kfd->rfd', lsel, lterm)
        rgot = xblocks[parts, send_block[:, p]].astype(f32) * live[:, p][:, None, None]
        rterm = jnp.einsum('qfs,qsd->qfd', rgot, rvals[p].astype(f32))
        rsel = (rem_dst[p][None, :] == rowids[:, None]).astype(f32)
        return total + jnp.einsum('rq,qfd->rfd', rsel, rterm)

    aggblocks = lax.map(gather_one, parts)
    agg = (aggblocks.transpose(2, 0, 1, 3).reshape(F, NODES) * mask[None, :]).astype(jnp.bfloat16)
    stacked = jnp.concatenate([xm, agg], axis=0)
    wflat = weight.reshape(2 * F, H)
    z = jnp.dot(wflat.T, stacked, preferred_element_type=f32) + bias[:, None]
    hidden = (jax.nn.silu(z) * mask[None, :]).astype(jnp.bfloat16)
    sig = jax.nn.sigmoid(z)
    dsilu = sig * (1.0 + z * (1.0 - sig))
    dz = (cot.astype(f32) * dsilu * mask[None, :]).astype(jnp.bfloat16)
    factor = 1.0 / (NODES ** 0.5)
    grad_weight = (jnp.dot(stacked, dz.T, preferred_element_type=f32) * factor).reshape(2, F, H)
    grad_bias = jnp.sum(dz.astype(f32), axis=1) * factor
    dx_all = jnp.dot(wflat, dz, preferred_element_type=f32)
    direct = dx_all[:F].astype(jnp.bfloat16)
    dagg = (dx_all[F:] * mask[None, :]).astype(jnp.bfloat16)
    gblocks = dagg.reshape(F, N_DOM, nblocks, BLK).transpose(1, 2, 0, 3)

    def scatter_one(d):
        lgot = gblocks[d][lcoord[d, :, 1]].astype(f32)
        lterm = jnp.einsum('kft,kst->kfs', lgot, lvals[d].astype(f32))
        lsel = (lcoord[d, :, 0][None, :] == rowids[:, None]).astype(f32)
        total = jnp.einsum('rk,kfs->rfs', lsel, lterm)
        rgot = gblocks[parts, rem_dst[:, d]].astype(f32)
        rterm = jnp.einsum('qft,qst->qfs', rgot, rvals[:, d].astype(f32)) * live[d][:, None, None]
        ssel = (send_block[d][None, :] == rowids[:, None]).astype(f32)
        return total + jnp.einsum('rq,qfs->rfs', ssel, rterm)

    backblocks = lax.map(scatter_one, parts)
    back = backblocks.transpose(2, 0, 1, 3).reshape(F, NODES)
    grad_feats = (direct.astype(f32) + back) * mask[None, :]
    return hidden, grad_feats, grad_weight, grad_bias
```

```python
import jax
import jax.numpy as jnp
from jax import lax
from jax.experimental import pallas as pl
from jax.experimental.pallas import tpu as pltpu
from jax.sharding import PartitionSpec as P

F32 = jnp.float32
BF16 = jnp.bfloat16
NX, NZ, NCORE = 4, 8, 2
NDOM = NX * NZ * NCORE
NCOL = 8
NB = 16
W = 128
ROWS = 16
H = 256
LOC = 24
CHUNK = 16

SMEM = pl.BlockSpec(memory_space=pltpu.SMEM)
VMEM = pl.BlockSpec(memory_space=pltpu.VMEM)
ANY = pl.BlockSpec(memory_space=pl.ANY)
NT = (((1,), (1,)), ((), ()))
NN = (((1,), (0,)), ((), ()))


def dot(a, b, dims=NN):
    return lax.dot_general(a, b, dims, preferred_element_type=F32)


def call(body, out_shape, in_specs, scratch=(), flops=0, nbytes=0, out_specs=None, name=None, aliases=None):
    many = isinstance(out_shape, (list, tuple))
    return pl.pallas_call(
        body,
        out_shape=out_shape,
        in_specs=in_specs,
        out_specs=out_specs or ([VMEM] * len(out_shape) if many else VMEM),
        scratch_shapes=list(scratch),
        compiler_params=pltpu.CompilerParams(vmem_limit_bytes=24 * 2**20),
        cost_estimate=pl.CostEstimate(flops=flops, bytes_accessed=nbytes, transcendentals=0),
        input_output_aliases=aliases or {},
        name=name,
    )


def masked_block(feats, live, b):
    node = lax.broadcasted_iota(jnp.int32, (ROWS, W), 1) + b * W
    return jnp.where(node < live, feats[:, b * W : (b + 1) * W].astype(F32), 0.0).astype(BF16)


def pick_kernel(live, send_block, send_live, feats, out, xs):
    for b in range(NB):
        xs[b] = masked_block(feats, live[0], b)
    xs[NB] = jnp.zeros((ROWS, W), BF16)
    for q in range(NDOM):
        out[q] = xs[jnp.where(send_live[0, q] > 0, send_block[0, q], NB)]


def start_chunks(hbm, buf, sems, total):
    copies = []
    for i in range(total // CHUNK):
        part = pl.ds(i * CHUNK, CHUNK)
        copy = pltpu.make_async_copy(hbm.at[part], buf.at[part], sems.at[i])
        copy.start()
        copies.append(copy)
    return copies


def local_fwd_kernel(live, coord, feats, vals, out, xs):
    for b in range(NB):
        xs[b] = masked_block(feats, live[0], b)
    out[...] = jnp.zeros_like(out)
    for k in range(LOC):
        out[coord[k, 1]] += dot(xs[coord[k, 0]], vals[k])


def agg_kernel(live, rem_dst, feats, arrived, local, rem, out, acc, buf, sems):
    copies = start_chunks(rem, buf, sems, NDOM)
    acc[...] = local[...]
    for c in range(NCOL):
        for j in range(2):
            out[c, 0:ROWS, j * W : (j + 1) * W] = masked_block(feats, live[0], 2 * c + j)
    for q in range(NDOM):
        if q % CHUNK == 0:
            copies[q // CHUNK].wait()
        acc[rem_dst[0, q]] += dot(arrived[q], buf[q])
    for c in range(NCOL):
        for j in range(2):
            b = 2 * c + j
            node = lax.broadcasted_iota(jnp.int32, (ROWS, W), 1) + b * W
            mask = (node < live[0]).astype(F32)
            out[c, ROWS : 2 * ROWS, j * W : (j + 1) * W] = (acc[b] * mask).astype(BF16)


def dense_kernel(live, first, got, wt, w, bias, cot, hidden, out):
    node = lax.broadcasted_iota(jnp.int32, (H, H), 1) + first[0]
    mask = (node < live[0]).astype(F32)
    x = got[...].reshape(NCOL * 2 * ROWS, H)
    z = dot(wt[...], x) + bias[...]
    sig = 1.0 / (1.0 + jnp.exp(-z))
    hidden[...] = (z * sig * mask).astype(BF16)
    dz = (cot[...].astype(F32) * (sig * (1.0 + z * (1.0 - sig))) * mask).astype(BF16)
    dx = dot(w[...], dz)
    dw = dot(x, dz, NT)
    db = dot(jnp.ones((ROWS, H), BF16), dz, NT)
    mask_rows = mask[0:ROWS]
    for c in range(NCOL):
        r = c * 2 * ROWS
        out[c, 0:ROWS] = dx[r : r + ROWS].astype(BF16)
        out[c, ROWS : 2 * ROWS] = (dx[r + ROWS : r + 2 * ROWS] * mask_rows).astype(BF16)
        out[c, 2 * ROWS : 4 * ROWS] = dw[r : r + 2 * ROWS].astype(BF16)
        out[c, 4 * ROWS : 5 * ROWS] = db.astype(BF16)


def dw_kernel(got, out):
    dw = jnp.zeros((2 * ROWS, H), F32)
    db = jnp.zeros((ROWS, H), F32)
    for c in range(NCOL):
        dw = dw + got[c, 2 * ROWS : 4 * ROWS].astype(F32)
        db = db + got[c, 4 * ROWS : 5 * ROWS].astype(F32)
    tail = jnp.concatenate([db[0:1, 0:W], db[0:1, W : 2 * W], jnp.zeros((6, W), F32)], axis=0)
    for r in range(4):
        for h in range(2):
            part = dw[8 * r : 8 * r + 8, h * W : (h + 1) * W]
            out[2 * r + h] = jnp.concatenate([part, tail], axis=0).astype(BF16)


def load_grad_blocks(got, gs):
    for c in range(NCOL):
        rows = got[c, ROWS : 2 * ROWS]
        gs[2 * c] = rows[:, 0:W]
        gs[2 * c + 1] = rows[:, W : 2 * W]


def back_kernel(rem_dst, got, rem, out, gs, buf, sems):
    copies = start_chunks(rem, buf, sems, NDOM)
    load_grad_blocks(got, gs)
    for q in range(NDOM):
        if q % CHUNK == 0:
            copies[q // CHUNK].wait()
        out[q, 0:ROWS] = dot(gs[rem_dst[0, q]], buf[q], NT).astype(BF16)


def attach_kernel(sent, got, out, buf, sem):
    total = jnp.zeros((ROWS, W), F32)
    for g in range(NX * NCORE):
        total = total + got[g].astype(F32)
    total = total.astype(BF16)
    for q in range(NDOM):
        buf[q] = total
    copy = pltpu.make_async_copy(buf, out.at[:, ROWS : 2 * ROWS, :], sem)
    copy.start()
    copy.wait()


def local_bwd_kernel(coord, got, vals, out, gs):
    load_grad_blocks(got, gs)
    for c in range(NCOL):
        rows = got[c, 0:ROWS].astype(F32)
        out[2 * c] = rows[:, 0:W]
        out[2 * c + 1] = rows[:, W : 2 * W]
    for k in range(LOC):
        out[coord[k, 0]] += dot(gs[coord[k, 1]], vals[k], NT)


def final_kernel(factor, live, send_block, send_live, local, got, grad, gw, gb, acc):
    acc[0:NB] = local[...]
    for q in range(NDOM):
        b = jnp.where(send_live[0, q] > 0, send_block[0, q], NB)
        acc[b] += got[q, 0:ROWS].astype(F32)
    for b in range(NB):
        node = lax.broadcasted_iota(jnp.int32, (ROWS, W), 1) + b * W
        mask = (node < live[0]).astype(F32)
        grad[:, b * W : (b + 1) * W] = acc[b] * mask
    for x in range(NX):
        for core in range(NCORE):
            total = jnp.zeros((ROWS, W), F32)
            for z in range(NZ):
                total = total + got[(x * NZ + z) * NCORE + core, ROWS : 2 * ROWS].astype(F32)
            total = total * factor
            r = 8 * (x % 2)
            gw[x // 2, r : r + 8, core * W : (core + 1) * W] = total[0:8]
            if x == 0 and core == 0:
                gb[...] = total[8:10]


def shards(
    feats,
    part_len,
    loc_vals,
    loc_coord,
    send_block,
    send_live,
    rem_vals,
    rem_dst,
    weight,
    bias,
    cot,
):
    sds = jax.ShapeDtypeStruct
    slots = feats.shape[1]
    first = (lax.axis_index("col") * (slots // NCOL)).astype(jnp.int32).reshape(1)
    groups = [[(x * NZ + z) * NCORE + core for x in range(NX) for core in range(NCORE)] for z in range(NZ)]
    wr = weight.reshape(2, NCOL, ROWS, H).transpose(1, 0, 2, 3).reshape(NCOL * 2 * ROWS, H)
    wt = wr.T
    factor = 1.0 / float(slots * NDOM) ** 0.5
    rem_scratch = [pltpu.VMEM((NDOM, W, W), BF16), pltpu.SemaphoreType.DMA((NDOM // CHUNK,))]
    rem_flops = 2 * NDOM * ROWS * W * W
    rem_bytes = NDOM * W * W * 2

    picked = call(
        pick_kernel,
        sds((NDOM, ROWS, W), BF16),
        [SMEM, SMEM, SMEM, VMEM],
        [pltpu.VMEM((NB + 1, ROWS, W), BF16)],
        nbytes=320 * 1024,
        name="pick",
    )(part_len, send_block, send_live, feats)
    arrived = lax.all_to_all(picked, "dom", split_axis=0, concat_axis=0, tiled=True)
    local = call(
        local_fwd_kernel,
        sds((NB, ROWS, W), F32),
        [SMEM, SMEM, VMEM, VMEM],
        [pltpu.VMEM((NB, ROWS, W), BF16)],
        flops=2 * LOC * ROWS * W * W,
        nbytes=LOC * W * W * 2,
        name="local_fwd",
    )(part_len, loc_coord, feats, loc_vals)
    stacked = call(
        agg_kernel,
        sds((NCOL, 2 * ROWS, 2 * W), BF16),
        [SMEM, SMEM, VMEM, VMEM, VMEM, ANY],
        [pltpu.VMEM((NB, ROWS, W), F32)] + rem_scratch,
        flops=rem_flops,
        nbytes=rem_bytes,
        name="agg",
    )(part_len, rem_dst, feats, arrived, local, rem_vals)
    regrouped = lax.all_to_all(stacked, "col", split_axis=0, concat_axis=0, tiled=True)
    hidden, outgoing = call(
        dense_kernel,
        [sds((H, 2 * W), BF16), sds((NCOL, 5 * ROWS, 2 * W), BF16)],
        [SMEM, SMEM] + [VMEM] * 5,
        flops=3 * 2 * H**3,
        nbytes=2**20,
        name="dense",
    )(part_len, first, regrouped, wt, wr, bias.reshape(H, 1), cot)
    returned = lax.all_to_all(outgoing, "col", split_axis=0, concat_axis=0, tiled=True)
    dw_send = call(dw_kernel, sds((NX * NCORE, ROWS, W), BF16), [VMEM], nbytes=400 * 1024, name="dw")(returned)
    dw_got = lax.all_to_all(
        dw_send, "dom", split_axis=0, concat_axis=0, tiled=True, axis_index_groups=groups
    )
    terms = call(
        back_kernel,
        sds((NDOM, 2 * ROWS, W), BF16),
        [SMEM, VMEM, ANY],
        [pltpu.VMEM((NB, ROWS, W), BF16)] + rem_scratch,
        flops=rem_flops,
        nbytes=rem_bytes,
        name="back",
    )(rem_dst, returned, rem_vals)
    terms = call(
        attach_kernel,
        sds((NDOM, 2 * ROWS, W), BF16),
        [ANY, VMEM],
        [pltpu.VMEM((NDOM, ROWS, W), BF16), pltpu.SemaphoreType.DMA],
        out_specs=ANY,
        nbytes=256 * 1024,
        aliases={0: 0},
        name="attach",
    )(terms, dw_got)
    got = lax.all_to_all(terms, "dom", split_axis=0, concat_axis=0, tiled=True)
    local_back = call(
        local_bwd_kernel,
        sds((NB, ROWS, W), F32),
        [SMEM, VMEM, VMEM],
        [pltpu.VMEM((NB, ROWS, W), BF16)],
        flops=2 * LOC * ROWS * W * W,
        nbytes=LOC * W * W * 2,
        name="local_bwd",
    )(loc_coord, returned, loc_vals)

    def final_body(*refs):
        final_kernel(factor, *refs)

    grad_feats, grad_weight, grad_bias = call(
        final_body,
        [sds((ROWS, slots), F32), sds((2, ROWS, H), F32), sds((2, W), F32)],
        [SMEM, SMEM, SMEM, VMEM, VMEM],
        [pltpu.VMEM((NB + 1, ROWS, W), F32)],
        nbytes=2**20,
        name="final",
    )(part_len, send_block, send_live, local_back, got)
    return (hidden, grad_feats, grad_weight, grad_bias.reshape(H))


def solution(mesh):
    placed = (
        P("col", "dom"),
        P("dom"),
        P("dom", None, None),
        P("dom", None),
        P("dom", None),
        P("dom", None),
        P("dom", None, None),
        P("dom", None),
        P(),
        P(),
        P(None, ("dom", "col")),
    )
    return jax.shard_map(
        shards,
        mesh=mesh,
        in_specs=placed,
        out_specs=(P(None, ("dom", "col")), P("col", "dom"), P(None, "col", None), P()),
        check_vma=False,
    )
```

```python
import jax
import jax.numpy as jnp
from jax import lax
from jax.experimental import pallas as pl
from jax.experimental.pallas import tpu as pltpu
from jax.sharding import PartitionSpec as P

F32 = jnp.float32
BF16 = jnp.bfloat16
NX, NZ, NCORE = 4, 8, 2
NDOM = NX * NZ * NCORE
NCOL = 8
NB = 16
W = 128
ROWS = 16
H = 256
LOC = 24
G = NX * NCORE
DW = NZ * ROWS
DB = DW + 4 * ROWS
TALL = DB + ROWS

SMEM = pl.BlockSpec(memory_space=pltpu.SMEM)
VMEM = pl.BlockSpec(memory_space=pltpu.VMEM)
ANY = pl.BlockSpec(memory_space=pl.ANY)
NT = (((1,), (1,)), ((), ()))
NN = (((1,), (0,)), ((), ()))


def dot(a, b, dims=NN):
    return lax.dot_general(a, b, dims, preferred_element_type=F32)


def call(body, out_shape, in_specs, scratch=(), flops=0, nbytes=0, name=None):
    many = isinstance(out_shape, (list, tuple))
    return pl.pallas_call(
        body,
        out_shape=out_shape,
        in_specs=in_specs,
        out_specs=[out_spec(s) for s in out_shape] if many else out_spec(out_shape),
        scratch_shapes=list(scratch),
        compiler_params=pltpu.CompilerParams(vmem_limit_bytes=24 * 2**20),
        cost_estimate=pl.CostEstimate(flops=flops, bytes_accessed=nbytes, transcendentals=0),
        name=name,
    )


def out_spec(shape):
    return SMEM if getattr(shape, "memory_space", None) == pltpu.SMEM else VMEM


def in_hbm(x):
    return pltpu.with_memory_space_constraint(x, pltpu.HBM)


def in_vmem(x):
    return pltpu.with_memory_space_constraint(x, pltpu.VMEM)


def masked_block(feats, live, b):
    node = lax.broadcasted_iota(jnp.int32, (ROWS, W), 1) + b * W
    return jnp.where(node < live, feats[:, b * W : (b + 1) * W].astype(F32), 0.0).astype(BF16)


def node_mask(live, b):
    node = lax.broadcasted_iota(jnp.int32, (ROWS, W), 1) + b * W
    return (node < live).astype(F32)


def pick_kernel(live, send_block, send_live, feats, out, xs):
    for b in range(NB):
        xs[b] = masked_block(feats, live[0], b)
    xs[NB] = jnp.zeros((ROWS, W), BF16)
    for q in range(NDOM):
        out[q] = xs[jnp.where(send_live[0, q] > 0, send_block[0, q], NB)]


def local_fwd_kernel(
    live, coord, rem_dst, send_block, send_live, feats, vals, rem, cot, local, xs, vals_here, rem_here, cot_here, places, sems
):
    copies = [
        pltpu.make_async_copy(vals, vals_here, sems.at[0]),
        pltpu.make_async_copy(rem, rem_here, sems.at[1]),
        pltpu.make_async_copy(cot, cot_here, sems.at[2]),
    ]
    for copy in copies:
        copy.start()
    for b in range(NB):
        xs[b] = masked_block(feats, live[0], b)
    local[...] = jnp.zeros_like(local)
    for q in range(NDOM):
        places[0, q] = rem_dst[0, q]
        places[1, q] = jnp.where(send_live[0, q] > 0, send_block[0, q], NB)
    for k in range(LOC):
        places[2, k] = coord[0, k]
        places[3, k] = coord[1, k]
    copies[0].wait()
    for k in range(LOC):
        local[coord[1, k]] += dot(xs[coord[0, k]], vals_here[k])
    copies[1].wait()
    copies[2].wait()


def agg_kernel(live, places, xs, arrived, local, rem, out, acc):
    acc[...] = local[...]
    for q in range(NDOM):
        acc[places[0, q]] += dot(arrived[q], rem[q])
    for c in range(NCOL):
        for j in range(2):
            b = 2 * c + j
            out[c, 0:ROWS, j * W : (j + 1) * W] = xs[b]
            out[c, ROWS : 2 * ROWS, j * W : (j + 1) * W] = (acc[b] * node_mask(live[0], b)).astype(BF16)


def dense_kernel(live, first, got, wt, w, bias, cot, hidden, out):
    node = lax.broadcasted_iota(jnp.int32, (H, H), 1) + first[0]
    mask = (node < live[0]).astype(F32)
    x = got[...].reshape(NCOL * 2 * ROWS, H)
    z = dot(wt[...], x) + bias[...]
    sig = 1.0 / (1.0 + jnp.exp(-z))
    hidden[...] = (z * sig * mask).astype(BF16)
    dz = (cot[...].astype(F32) * (sig * (1.0 + z * (1.0 - sig))) * mask).astype(BF16)
    dx = dot(w[...], dz)
    dw = dot(x, dz, NT)
    db = dot(jnp.ones((ROWS, H), BF16), dz, NT)
    mask_rows = mask[0:ROWS]
    for c in range(NCOL):
        r = c * 2 * ROWS
        out[c, 0:ROWS] = dx[r : r + ROWS].astype(BF16)
        out[c, ROWS : 2 * ROWS] = (dx[r + ROWS : r + 2 * ROWS] * mask_rows).astype(BF16)
        out[c, 2 * ROWS : 4 * ROWS] = dw[r : r + 2 * ROWS].astype(BF16)
        out[c, 4 * ROWS : 5 * ROWS] = db.astype(BF16)


def load_grad_blocks(got, gs):
    for c in range(NCOL):
        rows = got[c, ROWS : 2 * ROWS]
        gs[2 * c] = rows[:, 0:W]
        gs[2 * c + 1] = rows[:, W : 2 * W]


def back_kernel(places, got, rem, vals, out, local, gs):
    load_grad_blocks(got, gs)
    for c in range(NCOL):
        rows = got[c, 0:ROWS].astype(F32)
        local[2 * c] = rows[:, 0:W]
        local[2 * c + 1] = rows[:, W : 2 * W]
    dw = jnp.zeros((2 * ROWS, H), F32)
    db = jnp.zeros((ROWS, H), F32)
    for c in range(NCOL):
        dw = dw + got[c, 2 * ROWS : 4 * ROWS].astype(F32)
        db = db + got[c, 4 * ROWS : 5 * ROWS].astype(F32)
    dw = dw.astype(BF16)
    row = lax.broadcasted_iota(jnp.int32, (ROWS, W), 0)
    db = jnp.where(row == 0, db[:, 0:W], db[:, W : 2 * W]).astype(BF16)
    for g in range(G):
        out[g, DB:TALL] = db
        for h in range(2):
            out[g, DW + 2 * ROWS * h : DW + 2 * ROWS * (h + 1)] = dw[:, h * W : (h + 1) * W]
    for q in range(NDOM):
        x, z, core = q // (NZ * NCORE), q // NCORE % NZ, q % NCORE
        out[x * NCORE + core, z * ROWS : (z + 1) * ROWS] = dot(gs[places[0, q]], rem[q], NT).astype(BF16)
    for k in range(LOC):
        local[places[2, k]] += dot(gs[places[3, k]], vals[k], NT)


def turn_kernel(got, out):
    for g in range(G):
        for z in range(NZ):
            out[z, g * ROWS : (g + 1) * ROWS] = got[g, z * ROWS : (z + 1) * ROWS]
    total = got[0, DW:TALL].astype(F32)
    for g in range(1, G):
        total = total + got[g, DW:TALL].astype(F32)
    total = total.astype(BF16)
    for z in range(NZ):
        out[z, DW:TALL] = total


def final_kernel(factor, live, places, local, got, grad, gw, gb, acc):
    acc[0:NB] = local[...]
    for q in range(NDOM):
        x, z, core = q // (NZ * NCORE), q // NCORE % NZ, q % NCORE
        g = x * NCORE + core
        acc[places[1, q]] += got[z, g * ROWS : (g + 1) * ROWS].astype(F32)
    for b in range(NB):
        grad[:, b * W : (b + 1) * W] = acc[b] * node_mask(live[0], b)
    total = got[0, DW:TALL].astype(F32)
    for z in range(1, NZ):
        total = total + got[z, DW:TALL].astype(F32)
    total = total * factor
    for h in range(2):
        for t in range(2):
            r = 2 * ROWS * h + ROWS * t
            gw[t, :, h * W : (h + 1) * W] = total[r : r + ROWS]
    gb[...] = total[DB - DW : DB - DW + 2]


def shards(
    feats,
    part_len,
    loc_vals,
    loc_coord,
    send_block,
    send_live,
    rem_vals,
    rem_dst,
    weight,
    bias,
    cot,
):
    sds = jax.ShapeDtypeStruct
    slots = feats.shape[1]
    first = (lax.axis_index("col") * (slots // NCOL)).astype(jnp.int32).reshape(1)
    wr = weight.reshape(2, NCOL, ROWS, H).transpose(1, 0, 2, 3).reshape(NCOL * 2 * ROWS, H)
    wt = wr.T
    factor = 1.0 / float(slots * NDOM) ** 0.5
    at = lambda x, z, core: (x * NZ + z) * NCORE + core
    over_xcore = [[at(x, z, core) for x in range(NX) for core in range(NCORE)] for z in range(NZ)]
    over_z = [[at(x, z, core) for z in range(NZ)] for x in range(NX) for core in range(NCORE)]

    def swap(x, axis, groups=None):
        return lax.all_to_all(x, axis, split_axis=0, concat_axis=0, tiled=True, axis_index_groups=groups)

    picked = call(
        pick_kernel,
        sds((NDOM, ROWS, W), BF16),
        [SMEM, SMEM, SMEM, VMEM],
        [pltpu.VMEM((NB + 1, ROWS, W), BF16)],
        nbytes=320 * 1024,
        name="pick",
    )(part_len, in_hbm(send_block), in_hbm(send_live), in_hbm(feats))
    arrived = swap(picked, "dom")
    local, xs, vals_here, rem_here, cot_here, places = call(
        local_fwd_kernel,
        [
            pltpu.VMEM((NB, ROWS, W), F32),
            pltpu.VMEM((NB, ROWS, W), BF16),
            pltpu.VMEM(loc_vals.shape, BF16),
            pltpu.VMEM(rem_vals.shape, BF16),
            pltpu.VMEM(cot.shape, BF16),
            pltpu.SMEM((4, NDOM), jnp.int32),
        ],
        [SMEM, SMEM, SMEM, SMEM, SMEM, VMEM, ANY, ANY, ANY],
        [pltpu.SemaphoreType.DMA((3,))],
        flops=2 * LOC * ROWS * W * W,
        nbytes=4 * 2**20,
        name="local_fwd",
    )(
        part_len,
        in_hbm(loc_coord.T),
        in_hbm(rem_dst),
        in_hbm(send_block),
        in_hbm(send_live),
        in_hbm(feats),
        in_hbm(loc_vals),
        in_hbm(rem_vals),
        in_hbm(cot),
    )
    stacked = call(
        agg_kernel,
        sds((NCOL, 2 * ROWS, 2 * W), BF16),
        [SMEM, SMEM] + [VMEM] * 4,
        [pltpu.VMEM((NB, ROWS, W), F32)],
        flops=2 * NDOM * ROWS * W * W,
        nbytes=3 * 2**20,
        name="agg",
    )(part_len, places, xs, in_vmem(arrived), local, rem_here)
    regrouped = swap(stacked, "col")
    hidden, outgoing = call(
        dense_kernel,
        [sds((H, 2 * W), BF16), pltpu.VMEM((NCOL, 5 * ROWS, 2 * W), BF16)],
        [SMEM, SMEM] + [VMEM] * 5,
        flops=3 * 2 * H**3,
        nbytes=2**20,
        name="dense",
    )(part_len, first, in_vmem(regrouped), wt, wr, bias.reshape(H, 1), cot_here)
    returned = swap(outgoing, "col")
    terms, local_back = call(
        back_kernel,
        [pltpu.VMEM((G, TALL, W), BF16), pltpu.VMEM((NB, ROWS, W), F32)],
        [SMEM, VMEM, VMEM, VMEM],
        [pltpu.VMEM((NB, ROWS, W), BF16)],
        flops=2 * (NDOM + LOC) * ROWS * W * W,
        nbytes=4 * 2**20,
        name="back",
    )(places, in_vmem(returned), rem_here, vals_here)
    half = swap(terms, "dom", over_xcore)
    turned = call(
        turn_kernel,
        pltpu.VMEM((NZ, TALL, W), BF16),
        [VMEM],
        nbytes=2**20,
        name="turn",
    )(in_vmem(half))
    got = swap(turned, "dom", over_z)

    def final_body(*refs):
        final_kernel(factor, *refs)

    grad_feats, grad_weight, grad_bias = call(
        final_body,
        [sds((ROWS, slots), F32), sds((2, ROWS, H), F32), sds((2, W), F32)],
        [SMEM, SMEM, VMEM, VMEM],
        [pltpu.VMEM((NB + 1, ROWS, W), F32)],
        nbytes=2**20,
        name="final",
    )(part_len, places, local_back, in_vmem(got))
    return (hidden, grad_feats, grad_weight, grad_bias.reshape(H))


def solution(mesh):
    placed = (
        P("col", "dom"),
        P("dom"),
        P("dom", None, None),
        P("dom", None),
        P("dom", None),
        P("dom", None),
        P("dom", None, None),
        P("dom", None),
        P(),
        P(),
        P(None, ("dom", "col")),
    )
    return jax.shard_map(
        shards,
        mesh=mesh,
        in_specs=placed,
        out_specs=(P(None, ("dom", "col")), P("col", "dom"), P(None, "col", None), P()),
        check_vma=False,
    )
```

```python
import jax
import jax.numpy as jnp
from jax import lax
from jax.experimental import pallas as pl
from jax.experimental.pallas import tpu as pltpu
from jax.sharding import PartitionSpec as P

F32 = jnp.float32
BF16 = jnp.bfloat16
NX, NZ, NCORE = 4, 8, 2
NDOM = NX * NZ * NCORE
NCOL = 8
NB = 16
W = 128
ROWS = 16
H = 256
LOC = 24
WAYS = 4
PART = 16
G = NX * NCORE
DW = NZ * ROWS
DB = DW + 4 * ROWS
TALL = DB + ROWS
DIRECT, DAGG, DWS, DBS = 0, H, 2 * H, 4 * H
WIDE = DBS + W

SMEM = pl.BlockSpec(memory_space=pltpu.SMEM)
VMEM = pl.BlockSpec(memory_space=pltpu.VMEM)
ANY = pl.BlockSpec(memory_space=pl.ANY)
NT = (((1,), (1,)), ((), ()))
NN = (((1,), (0,)), ((), ()))


def dot(a, b, dims=NN):
    return lax.dot_general(a, b, dims, preferred_element_type=F32)


def call(body, out_shape, in_specs, scratch=(), flops=0, nbytes=0, name=None):
    many = isinstance(out_shape, (list, tuple))
    return pl.pallas_call(
        body,
        out_shape=out_shape,
        in_specs=in_specs,
        out_specs=[out_spec(s) for s in out_shape] if many else out_spec(out_shape),
        scratch_shapes=list(scratch),
        compiler_params=pltpu.CompilerParams(vmem_limit_bytes=8 * 2**20),
        cost_estimate=pl.CostEstimate(flops=flops, bytes_accessed=nbytes, transcendentals=0),
        name=name,
    )


def out_spec(shape):
    return {pltpu.SMEM: SMEM, pltpu.HBM: ANY}.get(getattr(shape, "memory_space", None), VMEM)


def in_hbm(x):
    return pltpu.with_memory_space_constraint(x, pltpu.HBM)


def in_vmem(x):
    return pltpu.with_memory_space_constraint(x, pltpu.VMEM)


def masked_block(feats, live, b):
    node = lax.broadcasted_iota(jnp.int32, (ROWS, W), 1) + b * W
    return jnp.where(node < live, feats[:, b * W : (b + 1) * W].astype(F32), 0.0).astype(BF16)


def node_mask(live, b):
    node = lax.broadcasted_iota(jnp.int32, (ROWS, W), 1) + b * W
    return (node < live).astype(F32)


def add_up(accs, b):
    total = accs[0][b]
    for acc in accs[1:]:
        total = total + acc[b]
    return total


def pick_kernel(live, send_block, send_live, feats, out, xs, buf, sems):
    for b in range(NB):
        xs[b] = masked_block(feats, live[0], b)
    xs[NB] = jnp.zeros((ROWS, W), BF16)
    copies = []
    for q in range(NDOM):
        buf[q] = xs[jnp.where(send_live[0, q] > 0, send_block[0, q], NB)]
        if q % PART == PART - 1:
            part = pl.ds(q + 1 - PART, PART)
            copies.append(pltpu.make_async_copy(buf.at[part], out.at[part], sems.at[q // PART]))
            copies[-1].start()
    for copy in copies:
        copy.wait()


def local_fwd_kernel(
    live, first, coord, rem_dst, send_block, send_live, feats, weight, bias, vals, rem, cot,
    local, xs, w_here, wt_here, bias_here, rem_here, cot_here, places, vals_here, sems,
):
    copies = [
        pltpu.make_async_copy(vals, vals_here, sems.at[0]),
        pltpu.make_async_copy(rem, rem_here, sems.at[1]),
        pltpu.make_async_copy(cot, cot_here, sems.at[2]),
    ]
    for copy in copies:
        copy.start()
    for c in range(NCOL):
        for t in range(2):
            r = (2 * c + t) * ROWS
            w_here[r : r + ROWS] = weight[t, c * ROWS : (c + 1) * ROWS]
    wt_here[...] = w_here[...].astype(F32).T.astype(BF16)
    bias_here[...] = jnp.broadcast_to(bias[...], (W, H)).T
    for b in range(NB):
        xs[b] = masked_block(feats, live[0], b)
    local[...] = jnp.zeros_like(local)
    for q in range(NDOM):
        places[0, q] = rem_dst[0, q]
        places[1, q] = jnp.where(send_live[0, q] > 0, send_block[0, q], NB)
    places[4, 0] = first[0]
    for k in range(LOC):
        places[2, k] = coord[0, k]
        places[3, k] = coord[1, k]
    copies[0].wait()
    for k in range(LOC):
        local[coord[1, k]] += dot(xs[coord[0, k]], vals_here[k])
    copies[1].wait()
    copies[2].wait()


def agg_kernel(live, places, xs, arrived, local, rem, out, *accs):
    accs[0][...] = local[...]
    for acc in accs[1:]:
        acc[...] = jnp.zeros_like(acc)
    for q in range(NDOM):
        accs[q % WAYS][places[0, q]] += dot(arrived[q], rem[q])
    for c in range(NCOL):
        for j in range(2):
            b = 2 * c + j
            out[c, 0:ROWS, j * W : (j + 1) * W] = xs[b]
            out[c, ROWS : 2 * ROWS, j * W : (j + 1) * W] = (add_up(accs, b) * node_mask(live[0], b)).astype(BF16)


def dense_kernel(live, places, got, wt, w, bias, cot, hidden, out):
    node = lax.broadcasted_iota(jnp.int32, (H, H), 1) + places[4, 0]
    mask = (node < live[0]).astype(F32)
    x = got[...].reshape(NCOL * 2 * ROWS, H)
    z = dot(wt[...], x) + jnp.concatenate([bias[...], bias[...]], axis=1)
    sig = 1.0 / (1.0 + jnp.exp(-z))
    hidden[...] = (z * sig * mask).astype(BF16)
    dz = (cot[...].astype(F32) * (sig * (1.0 + z * (1.0 - sig))) * mask).astype(BF16)
    dx = dot(w[...], dz)
    dw = dot(x, dz, NT)
    db = dot(jnp.ones((ROWS, H), BF16), dz, NT)
    mask_rows = mask[0:ROWS]
    row = lax.broadcasted_iota(jnp.int32, (ROWS, W), 0)
    db = jnp.where(row == 0, db[:, 0:W], db[:, W : 2 * W]).astype(BF16)
    for c in range(NCOL):
        r = c * 2 * ROWS
        out[c, :, DIRECT : DIRECT + H] = dx[r : r + ROWS].astype(BF16)
        out[c, :, DAGG : DAGG + H] = (dx[r + ROWS : r + 2 * ROWS] * mask_rows).astype(BF16)
        for t in range(2):
            out[c, :, DWS + t * H : DWS + (t + 1) * H] = dw[r + t * ROWS : r + (t + 1) * ROWS].astype(BF16)
        out[c, :, DBS : DBS + W] = db


def load_grad_blocks(got, gs):
    for c in range(NCOL):
        for j in range(2):
            gs[2 * c + j] = got[c, :, DAGG + j * W : DAGG + (j + 1) * W]


def back_kernel(places, got, rem, vals, hidden, out, local, hidden_out, gs, sem, *accs):
    copy = pltpu.make_async_copy(hidden, hidden_out, sem)
    copy.start()
    load_grad_blocks(got, gs)
    for c in range(NCOL):
        for j in range(2):
            accs[0][2 * c + j] = got[c, :, DIRECT + j * W : DIRECT + (j + 1) * W].astype(F32)
    for acc in accs[1:]:
        acc[...] = jnp.zeros_like(acc)
    sums = got[0, :, DWS : DBS + W].astype(F32)
    for c in range(1, NCOL):
        sums = sums + got[c, :, DWS : DBS + W].astype(F32)
    sums = sums.astype(BF16)
    for z in range(NZ):
        for i in range(5):
            r = DW + i * ROWS
            out[z, r : r + ROWS] = sums[:, i * W : (i + 1) * W]
    for q in range(NDOM):
        x, z, core = q // (NZ * NCORE), q // NCORE % NZ, q % NCORE
        g = x * NCORE + core
        out[z, g * ROWS : (g + 1) * ROWS] = dot(gs[places[0, q]], rem[q], NT).astype(BF16)
    for k in range(LOC):
        accs[k % WAYS][places[2, k]] += dot(gs[places[3, k]], vals[k], NT)
    for b in range(NB):
        local[b] = add_up(accs, b)
    copy.wait()


def turn_kernel(got, out):
    for g in range(G):
        for z in range(NZ):
            out[g, z * ROWS : (z + 1) * ROWS] = got[z, g * ROWS : (g + 1) * ROWS]
    total = got[0, DW:TALL].astype(F32)
    for z in range(1, NZ):
        total = total + got[z, DW:TALL].astype(F32)
    total = total.astype(BF16)
    for g in range(G):
        out[g, DW:TALL] = total


def final_kernel(factor, live, places, local, got, grad, gw, gb, *accs):
    accs[0][0:NB] = local[...]
    for acc in accs[1:]:
        acc[...] = jnp.zeros_like(acc)
    for q in range(NDOM):
        x, z, core = q // (NZ * NCORE), q // NCORE % NZ, q % NCORE
        g = x * NCORE + core
        accs[q % WAYS][places[1, q]] += got[g, z * ROWS : (z + 1) * ROWS].astype(F32)
    for b in range(NB):
        grad[:, b * W : (b + 1) * W] = add_up(accs, b) * node_mask(live[0], b)
    total = got[0, DW:TALL].astype(F32)
    for g in range(1, G):
        total = total + got[g, DW:TALL].astype(F32)
    total = total * factor
    for t in range(2):
        for h in range(2):
            r = (2 * t + h) * ROWS
            gw[t, :, h * W : (h + 1) * W] = total[r : r + ROWS]
    gb[...] = total[DB - DW : DB - DW + 2]


def shards(
    feats,
    part_len,
    loc_vals,
    loc_coord,
    send_block,
    send_live,
    rem_vals,
    rem_dst,
    weight,
    bias,
    cot,
):
    sds = jax.ShapeDtypeStruct
    slots = feats.shape[1]
    first = (lax.axis_index("col") * (slots // NCOL)).astype(jnp.int32).reshape(1)
    factor = 1.0 / float(slots * NDOM) ** 0.5
    at = lambda x, z, core: (x * NZ + z) * NCORE + core
    over_xcore = [[at(x, z, core) for x in range(NX) for core in range(NCORE)] for z in range(NZ)]
    over_z = [[at(x, z, core) for z in range(NZ)] for x in range(NX) for core in range(NCORE)]

    def swap(x, axis, groups=None):
        return lax.all_to_all(x, axis, split_axis=0, concat_axis=0, tiled=True, axis_index_groups=groups)

    picked = call(
        pick_kernel,
        pltpu.HBM((NDOM, ROWS, W), BF16),
        [SMEM, SMEM, SMEM, VMEM],
        [
            pltpu.VMEM((NB + 1, ROWS, W), BF16),
            pltpu.VMEM((NDOM, ROWS, W), BF16),
            pltpu.SemaphoreType.DMA((NDOM // PART,)),
        ],
        nbytes=320 * 1024,
        name="pick",
    )(part_len, in_hbm(send_block), in_hbm(send_live), in_hbm(feats))
    arrived = swap(picked, "dom")
    local, xs, w_here, wt_here, bias_here, rem_here, cot_here, places = call(
        local_fwd_kernel,
        [
            pltpu.VMEM((NB, ROWS, W), F32),
            pltpu.VMEM((NB, ROWS, W), BF16),
            pltpu.VMEM((H, H), BF16),
            pltpu.VMEM((H, H), BF16),
            pltpu.VMEM((H, W), F32),
            pltpu.VMEM(rem_vals.shape, BF16),
            pltpu.VMEM(cot.shape, BF16),
            pltpu.SMEM((5, NDOM), jnp.int32),
        ],
        [SMEM] * 6 + [VMEM] * 3 + [ANY] * 3,
        [pltpu.VMEM((LOC, W, W), BF16), pltpu.SemaphoreType.DMA((3,))],
        flops=2 * LOC * ROWS * W * W,
        nbytes=4 * 2**20,
        name="local_fwd",
    )(
        part_len,
        first,
        in_hbm(loc_coord.T),
        in_hbm(rem_dst),
        in_hbm(send_block),
        in_hbm(send_live),
        in_hbm(feats),
        in_hbm(weight),
        in_hbm(bias.reshape(1, H)),
        in_hbm(loc_vals),
        in_hbm(rem_vals),
        in_hbm(cot),
    )
    stacked = call(
        agg_kernel,
        pltpu.VMEM((NCOL, 2 * ROWS, 2 * W), BF16),
        [SMEM, SMEM] + [VMEM] * 4,
        [pltpu.VMEM((NB, ROWS, W), F32)] * WAYS,
        flops=2 * NDOM * ROWS * W * W,
        nbytes=3 * 2**20,
        name="agg",
    )(part_len, places, in_vmem(xs), in_vmem(arrived), in_vmem(local), in_vmem(rem_here))
    regrouped = swap(stacked, "col")
    hidden_here, outgoing = call(
        dense_kernel,
        [pltpu.VMEM((H, 2 * W), BF16), pltpu.VMEM((NCOL, ROWS, WIDE), BF16)],
        [SMEM, SMEM] + [VMEM] * 5,
        flops=3 * 2 * H**3,
        nbytes=2**20,
        name="dense",
    )(part_len, places, in_vmem(regrouped), in_vmem(wt_here), in_vmem(w_here), in_vmem(bias_here), in_vmem(cot_here))
    returned = swap(outgoing, "col")
    terms, local_back, hidden = call(
        back_kernel,
        [pltpu.VMEM((NZ, TALL, W), BF16), pltpu.VMEM((NB, ROWS, W), F32), pltpu.HBM((H, 2 * W), BF16)],
        [SMEM, VMEM, VMEM, VMEM, ANY],
        [pltpu.VMEM((NB, ROWS, W), BF16), pltpu.SemaphoreType.DMA] + [pltpu.VMEM((NB, ROWS, W), F32)] * WAYS,
        flops=2 * (NDOM + LOC) * ROWS * W * W,
        nbytes=4 * 2**20,
        name="back",
    )(places, in_vmem(returned), in_vmem(rem_here), in_vmem(loc_vals), in_vmem(hidden_here))
    half = swap(terms, "dom", over_z)
    turned = call(
        turn_kernel,
        pltpu.VMEM((G, TALL, W), BF16),
        [VMEM],
        nbytes=2**20,
        name="turn",
    )(in_vmem(half))
    got = swap(turned, "dom", over_xcore)

    def final_body(*refs):
        final_kernel(factor, *refs)

    grad_feats, grad_weight, grad_bias = call(
        final_body,
        [sds((ROWS, slots), F32), sds((2, ROWS, H), F32), sds((2, W), F32)],
        [SMEM, SMEM, VMEM, VMEM],
        [pltpu.VMEM((NB + 1, ROWS, W), F32)] * WAYS,
        nbytes=2**20,
        name="final",
    )(part_len, places, in_vmem(local_back), in_vmem(got))
    return (hidden, grad_feats, grad_weight, grad_bias.reshape(H))


def solution(mesh):
    placed = (
        P("col", "dom"),
        P("dom"),
        P("dom", None, None),
        P("dom", None),
        P("dom", None),
        P("dom", None),
        P("dom", None, None),
        P("dom", None),
        P(),
        P(),
        P(None, ("dom", "col")),
    )
    return jax.shard_map(
        shards,
        mesh=mesh,
        in_specs=placed,
        out_specs=(P(None, ("dom", "col")), P("col", "dom"), P(None, "col", None), P()),
        check_vma=False,
    )
```

```python
import jax
import jax.numpy as jnp
from jax import lax
from jax.experimental import pallas as pl
from jax.experimental.pallas import tpu as pltpu
from jax.sharding import PartitionSpec as P

F32 = jnp.float32
BF16 = jnp.bfloat16
NX, NZ, NCORE = 4, 8, 2
NDOM = NX * NZ * NCORE
NCOL = 8
NB = 16
W = 128
ROWS = 16
H = 256
LOC = 24
WAYS = 4
PART = 16
G = NX * NCORE
DW = NZ * ROWS
DB = DW + 4 * ROWS
TALL = DB + 8
DIRECT, DAGG, DWS, DBS = 0, 2 * ROWS, 4 * ROWS, 8 * ROWS
HIGH = DBS + 16

SMEM = pl.BlockSpec(memory_space=pltpu.SMEM)
VMEM = pl.BlockSpec(memory_space=pltpu.VMEM)
ANY = pl.BlockSpec(memory_space=pl.ANY)
NT = (((1,), (1,)), ((), ()))
NN = (((1,), (0,)), ((), ()))


def dot(a, b, dims=NN):
    return lax.dot_general(a, b, dims, preferred_element_type=F32)


def call(body, out_shape, in_specs, scratch=(), flops=0, nbytes=0, name=None):
    many = isinstance(out_shape, (list, tuple))
    return pl.pallas_call(
        body,
        out_shape=out_shape,
        in_specs=in_specs,
        out_specs=[out_spec(s) for s in out_shape] if many else out_spec(out_shape),
        scratch_shapes=list(scratch),
        compiler_params=pltpu.CompilerParams(vmem_limit_bytes=8 * 2**20),
        cost_estimate=pl.CostEstimate(flops=flops, bytes_accessed=nbytes, transcendentals=0),
        name=name,
    )


def out_spec(shape):
    return {pltpu.SMEM: SMEM, pltpu.HBM: ANY}.get(getattr(shape, "memory_space", None), VMEM)


def in_hbm(x):
    return pltpu.with_memory_space_constraint(x, pltpu.HBM)


def in_vmem(x):
    return pltpu.with_memory_space_constraint(x, pltpu.VMEM)


def masked_block(feats, live, b):
    node = lax.broadcasted_iota(jnp.int32, (ROWS, W), 1) + b * W
    return jnp.where(node < live, feats[:, b * W : (b + 1) * W].astype(F32), 0.0).astype(BF16)


def node_mask(live, b):
    node = lax.broadcasted_iota(jnp.int32, (ROWS, W), 1) + b * W
    return (node < live).astype(F32)


def add_up(accs, b):
    total = accs[0][b]
    for acc in accs[1:]:
        total = total + acc[b]
    return total


def pick_kernel(live, send_block, send_live, feats, out, xs, buf, sems):
    for b in range(NB):
        xs[b] = masked_block(feats, live[0], b)
    xs[NB] = jnp.zeros((ROWS, W), BF16)
    copies = []
    for q in range(NDOM):
        buf[q] = xs[jnp.where(send_live[0, q] > 0, send_block[0, q], NB)]
        if q % PART == PART - 1:
            part = pl.ds(q + 1 - PART, PART)
            copies.append(pltpu.make_async_copy(buf.at[part], out.at[part], sems.at[q // PART]))
            copies[-1].start()
    for copy in copies:
        copy.wait()


def local_fwd_kernel(
    live, first, coord, rem_dst, send_block, send_live, feats, weight, bias, vals, rem, cot,
    local, xs, w_here, wt_here, bias_here, rem_here, cot_here, places, rem_t, vals_t, vals_here, rem_buf, vals_buf, sems,
):
    copies = [
        pltpu.make_async_copy(vals, vals_here, sems.at[0]),
        pltpu.make_async_copy(rem, rem_here, sems.at[1]),
        pltpu.make_async_copy(cot, cot_here, sems.at[2]),
    ]
    for copy in copies:
        copy.start()
    for c in range(NCOL):
        for t in range(2):
            r = (2 * c + t) * ROWS
            w_here[r : r + ROWS] = weight[t, c * ROWS : (c + 1) * ROWS]
    wt_here[...] = w_here[...].astype(F32).T.astype(BF16)
    bias_here[...] = jnp.broadcast_to(bias[...], (W, H)).T
    for b in range(NB):
        xs[b] = masked_block(feats, live[0], b)
    local[...] = jnp.zeros_like(local)
    for q in range(NDOM):
        places[0, q] = rem_dst[0, q]
        places[1, q] = jnp.where(send_live[0, q] > 0, send_block[0, q], NB)
    places[4, 0] = first[0]
    for k in range(LOC):
        places[2, k] = coord[0, k]
        places[3, k] = coord[1, k]
    copies[0].wait()
    for k in range(LOC):
        local[coord[1, k]] += dot(xs[coord[0, k]], vals_here[k])
    for k in range(LOC):
        vals_buf[k] = vals_here[k].T
    copies[1].wait()
    copies.append(pltpu.make_async_copy(vals_buf, vals_t, sems.at[3]))
    copies[-1].start()
    for i in range(NDOM // PART):
        part = pl.ds(i * PART, PART)
        for q in range(i * PART, (i + 1) * PART):
            rem_buf[q] = rem_here[q].T
        copies.append(pltpu.make_async_copy(rem_buf.at[part], rem_t.at[part], sems.at[4 + i]))
        copies[-1].start()
    for copy in copies[2:]:
        copy.wait()


def agg_kernel(live, places, xs, arrived, local, rem, out, *accs):
    accs[0][...] = local[...]
    for acc in accs[1:]:
        acc[...] = jnp.zeros_like(acc)
    for q in range(NDOM):
        accs[q % WAYS][places[0, q]] += dot(arrived[q], rem[q])
    for c in range(NCOL):
        for j in range(2):
            b = 2 * c + j
            out[c, 0:ROWS, j * W : (j + 1) * W] = xs[b]
            out[c, ROWS : 2 * ROWS, j * W : (j + 1) * W] = (add_up(accs, b) * node_mask(live[0], b)).astype(BF16)


def dense_kernel(live, places, got, wt, w, bias, cot, hidden, out):
    node = lax.broadcasted_iota(jnp.int32, (H, H), 1) + places[4, 0]
    mask = (node < live[0]).astype(F32)
    x = got[...].reshape(NCOL * 2 * ROWS, H)
    z = dot(wt[...], x) + jnp.concatenate([bias[...], bias[...]], axis=1)
    sig = 1.0 / (1.0 + jnp.exp(-z))
    hidden[...] = (z * sig * mask).astype(BF16)
    dz = (cot[...].astype(F32) * (sig * (1.0 + z * (1.0 - sig))) * mask).astype(BF16)
    dx = dot(w[...], dz)
    dw = dot(x, dz, NT)
    db = dot(jnp.ones((ROWS, H), BF16), dz, NT)
    mask_rows = mask[0:ROWS]
    row = lax.broadcasted_iota(jnp.int32, (8, W), 0)
    db = jnp.where(row == 0, db[0:8, 0:W], db[0:8, W : 2 * W]).astype(BF16)
    for c in range(NCOL):
        r = c * 2 * ROWS
        direct = dx[r : r + ROWS].astype(BF16)
        dagg = (dx[r + ROWS : r + 2 * ROWS] * mask_rows).astype(BF16)
        for j in range(2):
            lanes = slice(j * W, (j + 1) * W)
            out[c, DIRECT + j * ROWS : DIRECT + (j + 1) * ROWS] = direct[:, lanes]
            out[c, DAGG + j * ROWS : DAGG + (j + 1) * ROWS] = dagg[:, lanes]
            for t in range(2):
                i = DWS + (2 * t + j) * ROWS
                out[c, i : i + ROWS] = dw[r + t * ROWS : r + (t + 1) * ROWS, lanes].astype(BF16)
        out[c, DBS:DBS + 8] = db


def load_grad_blocks(got, gs):
    for c in range(NCOL):
        for j in range(2):
            gs[2 * c + j] = got[c, DAGG + j * ROWS : DAGG + (j + 1) * ROWS]


def add_sums(got, start, middle, end, count):
    dw = got[0, start:middle].astype(F32)
    db = got[0, middle:end].astype(F32)
    for i in range(1, count):
        dw = dw + got[i, start:middle].astype(F32)
        db = db + got[i, middle:end].astype(F32)
    return dw, db


def back_kernel(places, got, rem, vals, hidden, out, local, hidden_out, gs, sem, *accs):
    copy = pltpu.make_async_copy(hidden, hidden_out, sem)
    copy.start()
    load_grad_blocks(got, gs)
    for c in range(NCOL):
        for j in range(2):
            accs[0][2 * c + j] = got[c, DIRECT + j * ROWS : DIRECT + (j + 1) * ROWS].astype(F32)
    for acc in accs[1:]:
        acc[...] = jnp.zeros_like(acc)
    dw, db = add_sums(got, DWS, DBS, DBS + 8, NCOL)
    for z in range(NZ):
        out[z, DW:DB] = dw.astype(BF16)
        out[z, DB:TALL] = db.astype(BF16)
    for q in range(NDOM):
        x, z, core = q // (NZ * NCORE), q // NCORE % NZ, q % NCORE
        g = x * NCORE + core
        out[z, g * ROWS : (g + 1) * ROWS] = dot(gs[places[0, q]], rem[q]).astype(BF16)
    for k in range(LOC):
        accs[k % WAYS][places[2, k]] += dot(gs[places[3, k]], vals[k])
    for b in range(NB):
        local[b] = add_up(accs, b)
    copy.wait()


def turn_kernel(got, out):
    for g in range(G):
        for z in range(NZ):
            out[g, z * ROWS : (z + 1) * ROWS] = got[z, g * ROWS : (g + 1) * ROWS]
    dw, db = add_sums(got, DW, DB, TALL, NZ)
    for g in range(G):
        out[g, DW:DB] = dw.astype(BF16)
        out[g, DB:TALL] = db.astype(BF16)


def final_kernel(factor, live, places, local, got, grad, gw, gb, *accs):
    accs[0][0:NB] = local[...]
    for acc in accs[1:]:
        acc[...] = jnp.zeros_like(acc)
    for q in range(NDOM):
        x, z, core = q // (NZ * NCORE), q // NCORE % NZ, q % NCORE
        g = x * NCORE + core
        accs[q % WAYS][places[1, q]] += got[g, z * ROWS : (z + 1) * ROWS].astype(F32)
    for b in range(NB):
        grad[:, b * W : (b + 1) * W] = add_up(accs, b) * node_mask(live[0], b)
    dw, db = add_sums(got, DW, DB, TALL, G)
    dw = dw * factor
    for t in range(2):
        for h in range(2):
            r = (2 * t + h) * ROWS
            gw[t, :, h * W : (h + 1) * W] = dw[r : r + ROWS]
    gb[...] = db[0:2] * factor


def shards(
    feats,
    part_len,
    loc_vals,
    loc_coord,
    send_block,
    send_live,
    rem_vals,
    rem_dst,
    weight,
    bias,
    cot,
):
    sds = jax.ShapeDtypeStruct
    slots = feats.shape[1]
    first = (lax.axis_index("col") * (slots // NCOL)).astype(jnp.int32).reshape(1)
    factor = 1.0 / float(slots * NDOM) ** 0.5
    at = lambda x, z, core: (x * NZ + z) * NCORE + core
    over_xcore = [[at(x, z, core) for x in range(NX) for core in range(NCORE)] for z in range(NZ)]
    over_z = [[at(x, z, core) for z in range(NZ)] for x in range(NX) for core in range(NCORE)]

    def swap(x, axis, groups=None):
        return lax.all_to_all(x, axis, split_axis=0, concat_axis=0, tiled=True, axis_index_groups=groups)

    picked = call(
        pick_kernel,
        pltpu.HBM((NDOM, ROWS, W), BF16),
        [SMEM, SMEM, SMEM, VMEM],
        [
            pltpu.VMEM((NB + 1, ROWS, W), BF16),
            pltpu.VMEM((NDOM, ROWS, W), BF16),
            pltpu.SemaphoreType.DMA((NDOM // PART,)),
        ],
        nbytes=320 * 1024,
        name="pick",
    )(part_len, in_hbm(send_block), in_hbm(send_live), in_hbm(feats))
    arrived = swap(picked, "dom")
    local, xs, w_here, wt_here, bias_here, rem_here, cot_here, places, rem_t, vals_t = call(
        local_fwd_kernel,
        [
            pltpu.VMEM((NB, ROWS, W), F32),
            pltpu.VMEM((NB, ROWS, W), BF16),
            pltpu.VMEM((H, H), BF16),
            pltpu.VMEM((H, H), BF16),
            pltpu.VMEM((H, W), F32),
            pltpu.VMEM(rem_vals.shape, BF16),
            pltpu.VMEM(cot.shape, BF16),
            pltpu.SMEM((5, NDOM), jnp.int32),
            pltpu.HBM(rem_vals.shape, BF16),
            pltpu.HBM(loc_vals.shape, BF16),
        ],
        [SMEM] * 6 + [VMEM] * 3 + [ANY] * 3,
        [
            pltpu.VMEM((LOC, W, W), BF16),
            pltpu.VMEM((NDOM, W, W), BF16),
            pltpu.VMEM((LOC, W, W), BF16),
            pltpu.SemaphoreType.DMA((4 + NDOM // PART,)),
        ],
        flops=2 * LOC * ROWS * W * W,
        nbytes=4 * 2**20,
        name="local_fwd",
    )(
        part_len,
        first,
        in_hbm(loc_coord.T),
        in_hbm(rem_dst),
        in_hbm(send_block),
        in_hbm(send_live),
        in_hbm(feats),
        in_hbm(weight),
        in_hbm(bias.reshape(1, H)),
        in_hbm(loc_vals),
        in_hbm(rem_vals),
        in_hbm(cot),
    )
    stacked = call(
        agg_kernel,
        pltpu.VMEM((NCOL, 2 * ROWS, 2 * W), BF16),
        [SMEM, SMEM] + [VMEM] * 4,
        [pltpu.VMEM((NB, ROWS, W), F32)] * WAYS,
        flops=2 * NDOM * ROWS * W * W,
        nbytes=3 * 2**20,
        name="agg",
    )(part_len, places, in_vmem(xs), in_vmem(arrived), in_vmem(local), in_vmem(rem_here))
    regrouped = swap(stacked, "col")
    hidden_here, outgoing = call(
        dense_kernel,
        [pltpu.VMEM((H, 2 * W), BF16), pltpu.VMEM((NCOL, HIGH, W), BF16)],
        [SMEM, SMEM] + [VMEM] * 5,
        flops=3 * 2 * H**3,
        nbytes=2**20,
        name="dense",
    )(part_len, places, in_vmem(regrouped), in_vmem(wt_here), in_vmem(w_here), in_vmem(bias_here), in_vmem(cot_here))
    returned = swap(outgoing, "col")
    terms, local_back, hidden = call(
        back_kernel,
        [pltpu.VMEM((NZ, TALL, W), BF16), pltpu.VMEM((NB, ROWS, W), F32), pltpu.HBM((H, 2 * W), BF16)],
        [SMEM, VMEM, VMEM, VMEM, ANY],
        [pltpu.VMEM((NB, ROWS, W), BF16), pltpu.SemaphoreType.DMA] + [pltpu.VMEM((NB, ROWS, W), F32)] * WAYS,
        flops=2 * (NDOM + LOC) * ROWS * W * W,
        nbytes=4 * 2**20,
        name="back",
    )(places, in_vmem(returned), in_vmem(rem_t), in_vmem(vals_t), in_vmem(hidden_here))
    half = swap(terms, "dom", over_z)
    turned = call(
        turn_kernel,
        pltpu.VMEM((G, TALL, W), BF16),
        [VMEM],
        nbytes=2**20,
        name="turn",
    )(in_vmem(half))
    got = swap(turned, "dom", over_xcore)

    def final_body(*refs):
        final_kernel(factor, *refs)

    grad_feats, grad_weight, grad_bias = call(
        final_body,
        [sds((ROWS, slots), F32), sds((2, ROWS, H), F32), sds((2, W), F32)],
        [SMEM, SMEM, VMEM, VMEM],
        [pltpu.VMEM((NB + 1, ROWS, W), F32)] * WAYS,
        nbytes=2**20,
        name="final",
    )(part_len, places, in_vmem(local_back), in_vmem(got))
    return (hidden, grad_feats, grad_weight, grad_bias.reshape(H))


def solution(mesh):
    placed = (
        P("col", "dom"),
        P("dom"),
        P("dom", None, None),
        P("dom", None),
        P("dom", None),
        P("dom", None),
        P("dom", None, None),
        P("dom", None),
        P(),
        P(),
        P(None, ("dom", "col")),
    )
    return jax.shard_map(
        shards,
        mesh=mesh,
        in_specs=placed,
        out_specs=(P(None, ("dom", "col")), P("col", "dom"), P(None, "col", None), P()),
        check_vma=False,
    )
```

```python
import jax
import jax.numpy as jnp
from jax import lax
from jax.experimental import pallas as pl
from jax.experimental.pallas import tpu as pltpu
from jax.sharding import PartitionSpec as P

F32 = jnp.float32
BF16 = jnp.bfloat16
NX, NZ, NCORE = 4, 8, 2
NDOM = NX * NZ * NCORE
NCOL = 8
NB = 16
W = 128
ROWS = 16
H = 256
LOC = 24
WAYS = 4
PART = 16
G = NX * NCORE
DW = NZ * ROWS
DB = DW + 4 * ROWS
TALL = DB + 8
DIRECT, DAGG, DWS, DBS = 0, 2 * ROWS, 4 * ROWS, 8 * ROWS
HIGH = DBS + 16

SMEM = pl.BlockSpec(memory_space=pltpu.SMEM)
VMEM = pl.BlockSpec(memory_space=pltpu.VMEM)
ANY = pl.BlockSpec(memory_space=pl.ANY)
NT = (((1,), (1,)), ((), ()))
NN = (((1,), (0,)), ((), ()))


def dot(a, b, dims=NN):
    return lax.dot_general(a, b, dims, preferred_element_type=F32)


def call(body, out_shape, in_specs, scratch=(), flops=0, nbytes=0, name=None):
    many = isinstance(out_shape, (list, tuple))
    return pl.pallas_call(
        body,
        out_shape=out_shape,
        in_specs=in_specs,
        out_specs=[out_spec(s) for s in out_shape] if many else out_spec(out_shape),
        scratch_shapes=list(scratch),
        compiler_params=pltpu.CompilerParams(vmem_limit_bytes=8 * 2**20),
        cost_estimate=pl.CostEstimate(flops=flops, bytes_accessed=nbytes, transcendentals=0),
        name=name,
    )


def out_spec(shape):
    return {pltpu.SMEM: SMEM, pltpu.HBM: ANY}.get(getattr(shape, "memory_space", None), VMEM)


def in_hbm(x):
    return pltpu.with_memory_space_constraint(x, pltpu.HBM)


def in_vmem(x):
    return pltpu.with_memory_space_constraint(x, pltpu.VMEM)


def masked_block(feats, live, b):
    node = lax.broadcasted_iota(jnp.int32, (ROWS, W), 1) + b * W
    return jnp.where(node < live, feats[:, b * W : (b + 1) * W].astype(F32), 0.0).astype(BF16)


def node_mask(live, b):
    node = lax.broadcasted_iota(jnp.int32, (ROWS, W), 1) + b * W
    return (node < live).astype(F32)


def add_up(accs, b):
    total = accs[0][b]
    for acc in accs[1:]:
        total = total + acc[b]
    return total


def pick_kernel(live, send_block, send_live, feats, out, xs, buf, sems):
    for b in range(NB):
        xs[b] = masked_block(feats, live[0], b)
    xs[NB] = jnp.zeros((ROWS, W), BF16)
    copies = []
    for q in range(NDOM):
        buf[q] = xs[jnp.where(send_live[0, q] > 0, send_block[0, q], NB)]
        if q % PART == PART - 1:
            part = pl.ds(q + 1 - PART, PART)
            copies.append(pltpu.make_async_copy(buf.at[part], out.at[part], sems.at[q // PART]))
            copies[-1].start()
    for copy in copies:
        copy.wait()


def local_fwd_kernel(
    live, first, coord, rem_dst, send_block, send_live, feats, weight, bias, vals, rem, cot,
    local, xs, w_here, wt_here, bias_here, rem_here, cot_here, places, rem_t, vals_t, vals_here, rem_buf, vals_buf, sems,
):
    copies = [
        pltpu.make_async_copy(vals, vals_here, sems.at[0]),
        pltpu.make_async_copy(rem, rem_here, sems.at[1]),
        pltpu.make_async_copy(cot, cot_here, sems.at[2]),
    ]
    for copy in copies:
        copy.start()
    for c in range(NCOL):
        for t in range(2):
            r = (2 * c + t) * ROWS
            w_here[r : r + ROWS] = weight[t, c * ROWS : (c + 1) * ROWS]
    wt_here[...] = w_here[...].astype(F32).T.astype(BF16)
    bias_here[...] = jnp.broadcast_to(bias[...], (W, H)).T
    for b in range(NB):
        xs[b] = masked_block(feats, live[0], b)
    local[...] = jnp.zeros_like(local)
    for q in range(NDOM):
        places[0, q] = rem_dst[0, q]
        places[1, q] = jnp.where(send_live[0, q] > 0, send_block[0, q], NB)
    places[4, 0] = first[0]
    for k in range(LOC):
        places[2, k] = coord[0, k]
        places[3, k] = coord[1, k]
    copies[0].wait()
    for k in range(LOC):
        local[coord[1, k]] += dot(xs[coord[0, k]], vals_here[k])
    for k in range(LOC):
        vals_buf[k] = vals_here[k].T
    copies[1].wait()
    copies.append(pltpu.make_async_copy(vals_buf, vals_t, sems.at[3]))
    copies[-1].start()
    for i in range(NDOM // PART):
        part = pl.ds(i * PART, PART)
        for q in range(i * PART, (i + 1) * PART):
            rem_buf[q] = rem_here[q].T
        copies.append(pltpu.make_async_copy(rem_buf.at[part], rem_t.at[part], sems.at[4 + i]))
        copies[-1].start()
    for copy in copies[2:]:
        copy.wait()


def agg_kernel(live, places, xs, arrived, local, rem, out, *accs):
    accs[0][...] = local[...]
    for acc in accs[1:]:
        acc[...] = jnp.zeros_like(acc)
    for q in range(NDOM):
        accs[q % WAYS][places[0, q]] += dot(arrived[q], rem[q])
    for c in range(NCOL):
        for j in range(2):
            b = 2 * c + j
            out[c, 0:ROWS, j * W : (j + 1) * W] = xs[b]
            out[c, ROWS : 2 * ROWS, j * W : (j + 1) * W] = (add_up(accs, b) * node_mask(live[0], b)).astype(BF16)


def dense_kernel(live, places, got, wt, w, bias, cot, hidden, out):
    node = lax.broadcasted_iota(jnp.int32, (H, H), 1) + places[4, 0]
    mask = (node < live[0]).astype(F32)
    x = got[...].reshape(NCOL * 2 * ROWS, H)
    z = dot(wt[...], x) + jnp.concatenate([bias[...], bias[...]], axis=1)
    sig = 1.0 / (1.0 + jnp.exp(-z))
    hidden[...] = (z * sig * mask).astype(BF16)
    dz = (cot[...].astype(F32) * (sig * (1.0 + z * (1.0 - sig))) * mask).astype(BF16)
    dx = dot(w[...], dz)
    dw = dot(x, dz, NT)
    db = dot(jnp.ones((ROWS, H), BF16), dz, NT)
    mask_rows = mask[0:ROWS]
    row = lax.broadcasted_iota(jnp.int32, (8, W), 0)
    db = jnp.where(row == 0, db[0:8, 0:W], db[0:8, W : 2 * W]).astype(BF16)
    for c in range(NCOL):
        r = c * 2 * ROWS
        direct = dx[r : r + ROWS].astype(BF16)
        dagg = (dx[r + ROWS : r + 2 * ROWS] * mask_rows).astype(BF16)
        for j in range(2):
            lanes = slice(j * W, (j + 1) * W)
            out[c, DIRECT + j * ROWS : DIRECT + (j + 1) * ROWS] = direct[:, lanes]
            out[c, DAGG + j * ROWS : DAGG + (j + 1) * ROWS] = dagg[:, lanes]
            for t in range(2):
                i = DWS + (2 * t + j) * ROWS
                out[c, i : i + ROWS] = dw[r + t * ROWS : r + (t + 1) * ROWS, lanes].astype(BF16)
        out[c, DBS:DBS + 8] = db


def load_grad_blocks(got, gs):
    for c in range(NCOL):
        for j in range(2):
            gs[2 * c + j] = got[c, DAGG + j * ROWS : DAGG + (j + 1) * ROWS]


def add_sums(got, start, middle, end, count):
    dw = got[0, start:middle].astype(F32)
    db = got[0, middle:end].astype(F32)
    for i in range(1, count):
        dw = dw + got[i, start:middle].astype(F32)
        db = db + got[i, middle:end].astype(F32)
    return dw, db


def back_kernel(places, got, rem, vals, hidden, out, local, hidden_out, gs, sem, *accs):
    copy = pltpu.make_async_copy(hidden, hidden_out, sem)
    copy.start()

    @pl.when(places[0, 0] >= 0)
    def _():
        back_body(places, got, rem, vals, out, local, gs, accs)

    copy.wait()


def back_body(places, got, rem, vals, out, local, gs, accs):
    load_grad_blocks(got, gs)
    for c in range(NCOL):
        for j in range(2):
            accs[0][2 * c + j] = got[c, DIRECT + j * ROWS : DIRECT + (j + 1) * ROWS].astype(F32)
    for acc in accs[1:]:
        acc[...] = jnp.zeros_like(acc)
    dw, db = add_sums(got, DWS, DBS, DBS + 8, NCOL)
    for z in range(NZ):
        out[z, DW:DB] = dw.astype(BF16)
        out[z, DB:TALL] = db.astype(BF16)
    for q in range(NDOM):
        x, z, core = q // (NZ * NCORE), q // NCORE % NZ, q % NCORE
        g = x * NCORE + core
        out[z, g * ROWS : (g + 1) * ROWS] = dot(gs[places[0, q]], rem[q]).astype(BF16)
    for k in range(LOC):
        accs[k % WAYS][places[2, k]] += dot(gs[places[3, k]], vals[k])
    for b in range(NB):
        local[b] = add_up(accs, b)


def turn_kernel(got, out):
    for g in range(G):
        for z in range(NZ):
            out[g, z * ROWS : (z + 1) * ROWS] = got[z, g * ROWS : (g + 1) * ROWS]
    dw, db = add_sums(got, DW, DB, TALL, NZ)
    for g in range(G):
        out[g, DW:DB] = dw.astype(BF16)
        out[g, DB:TALL] = db.astype(BF16)


def final_kernel(factor, live, places, local, got, grad, gw, gb, *accs):
    accs[0][0:NB] = local[...]
    for acc in accs[1:]:
        acc[...] = jnp.zeros_like(acc)
    for q in range(NDOM):
        x, z, core = q // (NZ * NCORE), q // NCORE % NZ, q % NCORE
        g = x * NCORE + core
        accs[q % WAYS][places[1, q]] += got[g, z * ROWS : (z + 1) * ROWS].astype(F32)
    for b in range(NB):
        grad[:, b * W : (b + 1) * W] = add_up(accs, b) * node_mask(live[0], b)
    dw, db = add_sums(got, DW, DB, TALL, G)
    dw = dw * factor
    for t in range(2):
        for h in range(2):
            r = (2 * t + h) * ROWS
            gw[t, :, h * W : (h + 1) * W] = dw[r : r + ROWS]
    gb[...] = db[0:2] * factor


def shards(
    feats,
    part_len,
    loc_vals,
    loc_coord,
    send_block,
    send_live,
    rem_vals,
    rem_dst,
    weight,
    bias,
    cot,
):
    sds = jax.ShapeDtypeStruct
    slots = feats.shape[1]
    first = (lax.axis_index("col") * (slots // NCOL)).astype(jnp.int32).reshape(1)
    factor = 1.0 / float(slots * NDOM) ** 0.5
    at = lambda x, z, core: (x * NZ + z) * NCORE + core
    over_xcore = [[at(x, z, core) for x in range(NX) for core in range(NCORE)] for z in range(NZ)]
    over_z = [[at(x, z, core) for z in range(NZ)] for x in range(NX) for core in range(NCORE)]

    def swap(x, axis, groups=None):
        return lax.all_to_all(x, axis, split_axis=0, concat_axis=0, tiled=True, axis_index_groups=groups)

    picked = call(
        pick_kernel,
        pltpu.HBM((NDOM, ROWS, W), BF16),
        [SMEM, SMEM, SMEM, VMEM],
        [
            pltpu.VMEM((NB + 1, ROWS, W), BF16),
            pltpu.VMEM((NDOM, ROWS, W), BF16),
            pltpu.SemaphoreType.DMA((NDOM // PART,)),
        ],
        nbytes=320 * 1024,
        name="pick",
    )(part_len, in_hbm(send_block), in_hbm(send_live), in_hbm(feats))
    arrived = swap(picked, "dom")
    local, xs, w_here, wt_here, bias_here, rem_here, cot_here, places, rem_t, vals_t = call(
        local_fwd_kernel,
        [
            pltpu.VMEM((NB, ROWS, W), F32),
            pltpu.VMEM((NB, ROWS, W), BF16),
            pltpu.VMEM((H, H), BF16),
            pltpu.VMEM((H, H), BF16),
            pltpu.VMEM((H, W), F32),
            pltpu.VMEM(rem_vals.shape, BF16),
            pltpu.VMEM(cot.shape, BF16),
            pltpu.SMEM((5, NDOM), jnp.int32),
            pltpu.HBM(rem_vals.shape, BF16),
            pltpu.HBM(loc_vals.shape, BF16),
        ],
        [SMEM] * 6 + [VMEM] * 3 + [ANY] * 3,
        [
            pltpu.VMEM((LOC, W, W), BF16),
            pltpu.VMEM((NDOM, W, W), BF16),
            pltpu.VMEM((LOC, W, W), BF16),
            pltpu.SemaphoreType.DMA((4 + NDOM // PART,)),
        ],
        flops=2 * LOC * ROWS * W * W,
        nbytes=4 * 2**20,
        name="local_fwd",
    )(
        part_len,
        first,
        in_hbm(loc_coord.T),
        in_hbm(rem_dst),
        in_hbm(send_block),
        in_hbm(send_live),
        in_hbm(feats),
        in_hbm(weight),
        in_hbm(bias.reshape(1, H)),
        in_hbm(loc_vals),
        in_hbm(rem_vals),
        in_hbm(cot),
    )
    stacked = call(
        agg_kernel,
        pltpu.VMEM((NCOL, 2 * ROWS, 2 * W), BF16),
        [SMEM, SMEM] + [VMEM] * 4,
        [pltpu.VMEM((NB, ROWS, W), F32)] * WAYS,
        flops=2 * NDOM * ROWS * W * W,
        nbytes=3 * 2**20,
        name="agg",
    )(part_len, places, in_vmem(xs), in_vmem(arrived), in_vmem(local), in_vmem(rem_here))
    regrouped = swap(stacked, "col")
    hidden_here, outgoing = call(
        dense_kernel,
        [pltpu.VMEM((H, 2 * W), BF16), pltpu.VMEM((NCOL, HIGH, W), BF16)],
        [SMEM, SMEM] + [VMEM] * 5,
        flops=3 * 2 * H**3,
        nbytes=2**20,
        name="dense",
    )(part_len, places, in_vmem(regrouped), in_vmem(wt_here), in_vmem(w_here), in_vmem(bias_here), in_vmem(cot_here))
    returned = swap(outgoing, "col")
    terms, local_back, hidden = call(
        back_kernel,
        [pltpu.VMEM((NZ, TALL, W), BF16), pltpu.VMEM((NB, ROWS, W), F32), pltpu.HBM((H, 2 * W), BF16)],
        [SMEM, VMEM, VMEM, VMEM, ANY],
        [pltpu.VMEM((NB, ROWS, W), BF16), pltpu.SemaphoreType.DMA] + [pltpu.VMEM((NB, ROWS, W), F32)] * WAYS,
        flops=2 * (NDOM + LOC) * ROWS * W * W,
        nbytes=4 * 2**20,
        name="back",
    )(places, in_vmem(returned), in_vmem(rem_t), in_vmem(vals_t), in_vmem(hidden_here))
    half = swap(terms, "dom", over_z)
    turned = call(
        turn_kernel,
        pltpu.VMEM((G, TALL, W), BF16),
        [VMEM],
        nbytes=2**20,
        name="turn",
    )(in_vmem(half))
    got = swap(turned, "dom", over_xcore)

    def final_body(*refs):
        final_kernel(factor, *refs)

    grad_feats, grad_weight, grad_bias = call(
        final_body,
        [sds((ROWS, slots), F32), sds((2, ROWS, H), F32), sds((2, W), F32)],
        [SMEM, SMEM, VMEM, VMEM],
        [pltpu.VMEM((NB + 1, ROWS, W), F32)] * WAYS,
        nbytes=2**20,
        name="final",
    )(part_len, places, in_vmem(local_back), in_vmem(got))
    return (hidden, grad_feats, grad_weight, grad_bias.reshape(H))


def solution(mesh):
    placed = (
        P("col", "dom"),
        P("dom"),
        P("dom", None, None),
        P("dom", None),
        P("dom", None),
        P("dom", None),
        P("dom", None, None),
        P("dom", None),
        P(),
        P(),
        P(None, ("dom", "col")),
    )
    return jax.shard_map(
        shards,
        mesh=mesh,
        in_specs=placed,
        out_specs=(P(None, ("dom", "col")), P("col", "dom"), P(None, "col", None), P()),
        check_vma=False,
    )
```

```python
import jax
import jax.numpy as jnp
from jax import lax
from jax.experimental import pallas as pl
from jax.experimental.pallas import tpu as pltpu
from jax.sharding import PartitionSpec as P

F32 = jnp.float32
BF16 = jnp.bfloat16
NX, NZ, NCORE = 4, 8, 2
NDOM = NX * NZ * NCORE
NCOL = 8
NB = 16
W = 128
ROWS = 16
H = 256
LOC = 24
WAYS = 4
PART = 16
G = NX * NCORE
DW = NZ * ROWS
DB = DW + 4 * ROWS
TALL = DB + 8
DIRECT, DAGG, DWS, DBS = 0, 2 * ROWS, 4 * ROWS, 8 * ROWS
HIGH = DBS + 8

SMEM = pl.BlockSpec(memory_space=pltpu.SMEM)
VMEM = pl.BlockSpec(memory_space=pltpu.VMEM)
ANY = pl.BlockSpec(memory_space=pl.ANY)
NT = (((1,), (1,)), ((), ()))
NN = (((1,), (0,)), ((), ()))


def dot(a, b, dims=NN):
    return lax.dot_general(a, b, dims, preferred_element_type=F32)


def call(body, out_shape, in_specs, scratch=(), flops=0, nbytes=0, name=None):
    many = isinstance(out_shape, (list, tuple))
    return pl.pallas_call(
        body,
        out_shape=out_shape,
        in_specs=in_specs,
        out_specs=[out_spec(s) for s in out_shape] if many else out_spec(out_shape),
        scratch_shapes=list(scratch),
        compiler_params=pltpu.CompilerParams(vmem_limit_bytes=8 * 2**20),
        cost_estimate=pl.CostEstimate(flops=flops, bytes_accessed=nbytes, transcendentals=0),
        name=name,
    )


def out_spec(shape):
    return {pltpu.SMEM: SMEM, pltpu.HBM: ANY}.get(getattr(shape, "memory_space", None), VMEM)


def in_hbm(x):
    return pltpu.with_memory_space_constraint(x, pltpu.HBM)


def in_vmem(x):
    return pltpu.with_memory_space_constraint(x, pltpu.VMEM)


def masked_block(feats, live, b):
    node = lax.broadcasted_iota(jnp.int32, (ROWS, W), 1) + b * W
    return jnp.where(node < live, feats[:, b * W : (b + 1) * W].astype(F32), 0.0).astype(BF16)


def node_mask(live, b):
    node = lax.broadcasted_iota(jnp.int32, (ROWS, W), 1) + b * W
    return (node < live).astype(F32)


def add_up(accs, b):
    total = accs[0][b]
    for acc in accs[1:]:
        total = total + acc[b]
    return total


def pick_kernel(live, send_block, send_live, feats, out, xs, buf, sems):
    for b in range(NB):
        xs[b] = masked_block(feats, live[0], b)
    xs[NB] = jnp.zeros((ROWS, W), BF16)
    copies = []
    for q in range(NDOM):
        buf[q] = xs[jnp.where(send_live[0, q] > 0, send_block[0, q], NB)]
        if q % PART == PART - 1:
            part = pl.ds(q + 1 - PART, PART)
            copies.append(pltpu.make_async_copy(buf.at[part], out.at[part], sems.at[q // PART]))
            copies[-1].start()
    for copy in copies:
        copy.wait()


def local_fwd_kernel(
    live, first, coord, rem_dst, send_block, send_live, feats, weight, bias, vals, rem, cot,
    local, xs, w_here, wt_here, bias_here, rem_here, cot_here, places, rem_t, vals_t, vals_here, rem_buf, vals_buf, sems,
):
    copies = [
        pltpu.make_async_copy(vals, vals_here, sems.at[0]),
        pltpu.make_async_copy(rem, rem_here, sems.at[1]),
        pltpu.make_async_copy(cot, cot_here, sems.at[2]),
    ]
    for copy in copies:
        copy.start()
    for c in range(NCOL):
        for t in range(2):
            r = (2 * c + t) * ROWS
            w_here[r : r + ROWS] = weight[t, c * ROWS : (c + 1) * ROWS]
    wt_here[...] = w_here[...].astype(F32).T.astype(BF16)
    bias_here[...] = jnp.broadcast_to(bias[...], (W, H)).T
    for b in range(NB):
        xs[b] = masked_block(feats, live[0], b)
    local[...] = jnp.zeros_like(local)
    for q in range(NDOM):
        places[0, q] = rem_dst[0, q]
        places[1, q] = jnp.where(send_live[0, q] > 0, send_block[0, q], NB)
    places[4, 0] = first[0]
    for k in range(LOC):
        places[2, k] = coord[0, k]
        places[3, k] = coord[1, k]
    copies[0].wait()
    for k in range(LOC):
        local[coord[1, k]] += dot(xs[coord[0, k]], vals_here[k])
    for k in range(LOC):
        vals_buf[k] = vals_here[k].T
    copies[1].wait()
    copies.append(pltpu.make_async_copy(vals_buf, vals_t, sems.at[3]))
    copies[-1].start()
    for i in range(NDOM // PART):
        part = pl.ds(i * PART, PART)
        for q in range(i * PART, (i + 1) * PART):
            rem_buf[q] = rem_here[q].T
        copies.append(pltpu.make_async_copy(rem_buf.at[part], rem_t.at[part], sems.at[4 + i]))
        copies[-1].start()
    for copy in copies[2:]:
        copy.wait()


def agg_kernel(live, places, xs, arrived, local, rem, out, *accs):
    accs[0][...] = local[...]
    for acc in accs[1:]:
        acc[...] = jnp.zeros_like(acc)
    for q in range(NDOM):
        accs[q % WAYS][places[0, q]] += dot(arrived[q], rem[q])
    for c in range(NCOL):
        for j in range(2):
            b = 2 * c + j
            out[c, 0:ROWS, j * W : (j + 1) * W] = xs[b]
            out[c, ROWS : 2 * ROWS, j * W : (j + 1) * W] = (add_up(accs, b) * node_mask(live[0], b)).astype(BF16)


def dense_kernel(live, places, got, wt, w, bias, cot, hidden, out):
    node = lax.broadcasted_iota(jnp.int32, (H, H), 1) + places[4, 0]
    mask = (node < live[0]).astype(F32)
    x = got[...].reshape(NCOL * 2 * ROWS, H)
    z = dot(wt[...], x) + jnp.concatenate([bias[...], bias[...]], axis=1)
    sig = 1.0 / (1.0 + jnp.exp(-z))
    hidden[...] = (z * sig * mask).astype(BF16)
    dz = (cot[...].astype(F32) * (sig * (1.0 + z * (1.0 - sig))) * mask).astype(BF16)
    dx = dot(w[...], dz)
    dw = dot(x, dz, NT)
    db = dot(jnp.ones((ROWS, H), BF16), dz, NT)
    mask_rows = mask[0:ROWS]
    row = lax.broadcasted_iota(jnp.int32, (8, W), 0)
    db = jnp.where(row == 0, db[0:8, 0:W], db[0:8, W : 2 * W]).astype(BF16)
    for c in range(NCOL):
        r = c * 2 * ROWS
        direct = dx[r : r + ROWS].astype(BF16)
        dagg = (dx[r + ROWS : r + 2 * ROWS] * mask_rows).astype(BF16)
        for j in range(2):
            lanes = slice(j * W, (j + 1) * W)
            out[c, DIRECT + j * ROWS : DIRECT + (j + 1) * ROWS] = direct[:, lanes]
            out[c, DAGG + j * ROWS : DAGG + (j + 1) * ROWS] = dagg[:, lanes]
            for t in range(2):
                i = DWS + (2 * t + j) * ROWS
                out[c, i : i + ROWS] = dw[r + t * ROWS : r + (t + 1) * ROWS, lanes].astype(BF16)
        out[c, DBS:DBS + 8] = db


def load_grad_blocks(got, gs):
    for c in range(NCOL):
        for j in range(2):
            gs[2 * c + j] = got[c, DAGG + j * ROWS : DAGG + (j + 1) * ROWS]


def add_sums(got, start, middle, end, count):
    dw = got[0, start:middle].astype(F32)
    db = got[0, middle:end].astype(F32)
    for i in range(1, count):
        dw = dw + got[i, start:middle].astype(F32)
        db = db + got[i, middle:end].astype(F32)
    return dw, db


def back_kernel(places, got, rem, vals, hidden, out, local, hidden_out, gs, sem, *accs):
    copy = pltpu.make_async_copy(hidden, hidden_out, sem)
    copy.start()

    @pl.when(places[0, 0] >= 0)
    def _():
        back_body(places, got, rem, vals, out, local, gs, accs)

    copy.wait()


def back_body(places, got, rem, vals, out, local, gs, accs):
    load_grad_blocks(got, gs)
    for c in range(NCOL):
        for j in range(2):
            accs[0][2 * c + j] = got[c, DIRECT + j * ROWS : DIRECT + (j + 1) * ROWS].astype(F32)
    for acc in accs[1:]:
        acc[...] = jnp.zeros_like(acc)
    dw, db = add_sums(got, DWS, DBS, DBS + 8, NCOL)
    for z in range(NZ):
        out[z, DW:DB] = dw.astype(BF16)
        out[z, DB:TALL] = db.astype(BF16)
    for q in range(NDOM):
        x, z, core = q // (NZ * NCORE), q // NCORE % NZ, q % NCORE
        g = x * NCORE + core
        out[z, g * ROWS : (g + 1) * ROWS] = dot(gs[places[0, q]], rem[q]).astype(BF16)
    for k in range(LOC):
        accs[k % WAYS][places[2, k]] += dot(gs[places[3, k]], vals[k])
    for b in range(NB):
        local[b] = add_up(accs, b)


def turn_kernel(got, out):
    for g in range(G):
        for z in range(NZ):
            out[g, z * ROWS : (z + 1) * ROWS] = got[z, g * ROWS : (g + 1) * ROWS]
    dw, db = add_sums(got, DW, DB, TALL, NZ)
    for g in range(G):
        out[g, DW:DB] = dw.astype(BF16)
        out[g, DB:TALL] = db.astype(BF16)


def final_kernel(factor, live, places, local, got, grad, gw, gb, *accs):
    accs[0][0:NB] = local[...]
    for acc in accs[1:]:
        acc[...] = jnp.zeros_like(acc)
    for q in range(NDOM):
        x, z, core = q // (NZ * NCORE), q // NCORE % NZ, q % NCORE
        g = x * NCORE + core
        accs[q % WAYS][places[1, q]] += got[g, z * ROWS : (z + 1) * ROWS].astype(F32)
    for b in range(NB):
        grad[:, b * W : (b + 1) * W] = add_up(accs, b) * node_mask(live[0], b)
    dw, db = add_sums(got, DW, DB, TALL, G)
    dw = dw * factor
    for t in range(2):
        for h in range(2):
            r = (2 * t + h) * ROWS
            gw[t, :, h * W : (h + 1) * W] = dw[r : r + ROWS]
    gb[...] = db[0:2] * factor


def shards(
    feats,
    part_len,
    loc_vals,
    loc_coord,
    send_block,
    send_live,
    rem_vals,
    rem_dst,
    weight,
    bias,
    cot,
):
    sds = jax.ShapeDtypeStruct
    slots = feats.shape[1]
    first = (lax.axis_index("col") * (slots // NCOL)).astype(jnp.int32).reshape(1)
    factor = 1.0 / float(slots * NDOM) ** 0.5
    at = lambda x, z, core: (x * NZ + z) * NCORE + core
    over_xcore = [[at(x, z, core) for x in range(NX) for core in range(NCORE)] for z in range(NZ)]
    over_z = [[at(x, z, core) for z in range(NZ)] for x in range(NX) for core in range(NCORE)]

    def swap(x, axis, groups=None):
        return lax.all_to_all(x, axis, split_axis=0, concat_axis=0, tiled=True, axis_index_groups=groups)

    picked = call(
        pick_kernel,
        pltpu.HBM((NDOM, ROWS, W), BF16),
        [SMEM, SMEM, SMEM, VMEM],
        [
            pltpu.VMEM((NB + 1, ROWS, W), BF16),
            pltpu.VMEM((NDOM, ROWS, W), BF16),
            pltpu.SemaphoreType.DMA((NDOM // PART,)),
        ],
        nbytes=320 * 1024,
        name="pick",
    )(part_len, in_hbm(send_block), in_hbm(send_live), in_hbm(feats))
    arrived = swap(picked, "dom")
    local, xs, w_here, wt_here, bias_here, rem_here, cot_here, places, rem_t, vals_t = call(
        local_fwd_kernel,
        [
            pltpu.VMEM((NB, ROWS, W), F32),
            pltpu.VMEM((NB, ROWS, W), BF16),
            pltpu.VMEM((H, H), BF16),
            pltpu.VMEM((H, H), BF16),
            pltpu.VMEM((H, W), F32),
            pltpu.VMEM(rem_vals.shape, BF16),
            pltpu.VMEM(cot.shape, BF16),
            pltpu.SMEM((5, NDOM), jnp.int32),
            pltpu.HBM(rem_vals.shape, BF16),
            pltpu.HBM(loc_vals.shape, BF16),
        ],
        [SMEM] * 6 + [VMEM] * 3 + [ANY] * 3,
        [
            pltpu.VMEM((LOC, W, W), BF16),
            pltpu.VMEM((NDOM, W, W), BF16),
            pltpu.VMEM((LOC, W, W), BF16),
            pltpu.SemaphoreType.DMA((4 + NDOM // PART,)),
        ],
        flops=2 * LOC * ROWS * W * W,
        nbytes=4 * 2**20,
        name="local_fwd",
    )(
        part_len,
        first,
        in_hbm(loc_coord.T),
        in_hbm(rem_dst),
        in_hbm(send_block),
        in_hbm(send_live),
        in_hbm(feats),
        in_hbm(weight),
        in_hbm(bias.reshape(1, H)),
        in_hbm(loc_vals),
        in_hbm(rem_vals),
        in_hbm(cot),
    )
    stacked = call(
        agg_kernel,
        pltpu.VMEM((NCOL, 2 * ROWS, 2 * W), BF16),
        [SMEM, SMEM] + [VMEM] * 4,
        [pltpu.VMEM((NB, ROWS, W), F32)] * WAYS,
        flops=2 * NDOM * ROWS * W * W,
        nbytes=3 * 2**20,
        name="agg",
    )(part_len, places, in_vmem(xs), in_vmem(arrived), in_vmem(local), in_vmem(rem_here))
    regrouped = swap(stacked, "col")
    hidden_here, outgoing = call(
        dense_kernel,
        [pltpu.VMEM((H, 2 * W), BF16), pltpu.VMEM((NCOL, HIGH, W), BF16)],
        [SMEM, SMEM] + [VMEM] * 5,
        flops=3 * 2 * H**3,
        nbytes=2**20,
        name="dense",
    )(part_len, places, in_vmem(regrouped), in_vmem(wt_here), in_vmem(w_here), in_vmem(bias_here), in_vmem(cot_here))
    returned = swap(outgoing.reshape(NCOL, HIGH // 8, 8, W), "col").reshape(NCOL, HIGH, W)
    terms, local_back, hidden = call(
        back_kernel,
        [pltpu.VMEM((NZ, TALL, W), BF16), pltpu.VMEM((NB, ROWS, W), F32), pltpu.HBM((H, 2 * W), BF16)],
        [SMEM, VMEM, VMEM, VMEM, ANY],
        [pltpu.VMEM((NB, ROWS, W), BF16), pltpu.SemaphoreType.DMA] + [pltpu.VMEM((NB, ROWS, W), F32)] * WAYS,
        flops=2 * (NDOM + LOC) * ROWS * W * W,
        nbytes=4 * 2**20,
        name="back",
    )(places, in_vmem(returned), in_vmem(rem_t), in_vmem(vals_t), in_vmem(hidden_here))
    half = swap(terms, "dom", over_z)
    turned = call(
        turn_kernel,
        pltpu.VMEM((G, TALL, W), BF16),
        [VMEM],
        nbytes=2**20,
        name="turn",
    )(in_vmem(half))
    got = swap(turned, "dom", over_xcore)

    def final_body(*refs):
        final_kernel(factor, *refs)

    grad_feats, grad_weight, grad_bias = call(
        final_body,
        [sds((ROWS, slots), F32), sds((2, ROWS, H), F32), sds((2, W), F32)],
        [SMEM, SMEM, VMEM, VMEM],
        [pltpu.VMEM((NB + 1, ROWS, W), F32)] * WAYS,
        nbytes=2**20,
        name="final",
    )(part_len, places, in_vmem(local_back), in_vmem(got))
    return (hidden, grad_feats, grad_weight, grad_bias.reshape(H))


def solution(mesh):
    placed = (
        P("col", "dom"),
        P("dom"),
        P("dom", None, None),
        P("dom", None),
        P("dom", None),
        P("dom", None),
        P("dom", None, None),
        P("dom", None),
        P(),
        P(),
        P(None, ("dom", "col")),
    )
    return jax.shard_map(
        shards,
        mesh=mesh,
        in_specs=placed,
        out_specs=(P(None, ("dom", "col")), P("col", "dom"), P(None, "col", None), P()),
        check_vma=False,
    )
```

```python
import jax
import jax.numpy as jnp
from jax import lax
from jax.experimental import pallas as pl
from jax.experimental.pallas import tpu as pltpu
from jax.sharding import PartitionSpec as P

F32 = jnp.float32
BF16 = jnp.bfloat16
NX, NZ, NCORE = 4, 8, 2
NDOM = NX * NZ * NCORE
NCOL = 8
NB = 16
W = 128
ROWS = 16
H = 256
LOC = 24
WAYS = 4
PART = 16
G = NX * NCORE
DW = NZ * ROWS
DB = DW + 4 * ROWS
TALL = DB + 8
DIRECT, DAGG, DWS, DBS = 0, 2 * ROWS, 4 * ROWS, 8 * ROWS
HIGH = DBS + 8

SMEM = pl.BlockSpec(memory_space=pltpu.SMEM)
VMEM = pl.BlockSpec(memory_space=pltpu.VMEM)
ANY = pl.BlockSpec(memory_space=pl.ANY)
NT = (((1,), (1,)), ((), ()))
NN = (((1,), (0,)), ((), ()))


def dot(a, b, dims=NN):
    return lax.dot_general(a, b, dims, preferred_element_type=F32)


def call(body, out_shape, in_specs, scratch=(), flops=0, nbytes=0, name=None):
    many = isinstance(out_shape, (list, tuple))
    return pl.pallas_call(
        body,
        out_shape=out_shape,
        in_specs=in_specs,
        out_specs=[out_spec(s) for s in out_shape] if many else out_spec(out_shape),
        scratch_shapes=list(scratch),
        compiler_params=pltpu.CompilerParams(vmem_limit_bytes=8 * 2**20),
        cost_estimate=pl.CostEstimate(flops=flops, bytes_accessed=nbytes, transcendentals=0),
        name=name,
    )


def out_spec(shape):
    return {pltpu.SMEM: SMEM, pltpu.HBM: ANY}.get(getattr(shape, "memory_space", None), VMEM)


def in_hbm(x):
    return pltpu.with_memory_space_constraint(x, pltpu.HBM)


def in_vmem(x):
    return pltpu.with_memory_space_constraint(x, pltpu.VMEM)


def masked_block(feats, live, b):
    node = lax.broadcasted_iota(jnp.int32, (ROWS, W), 1) + b * W
    return jnp.where(node < live, feats[:, b * W : (b + 1) * W].astype(F32), 0.0).astype(BF16)


def node_mask(live, b):
    node = lax.broadcasted_iota(jnp.int32, (ROWS, W), 1) + b * W
    return (node < live).astype(F32)


def add_up(accs, b):
    total = accs[0][b]
    for acc in accs[1:]:
        total = total + acc[b]
    return total


def pick_kernel(live, send_block, send_live, feats, out, xs, buf, sems):
    for b in range(NB):
        xs[b] = masked_block(feats, live[0], b)
    xs[NB] = jnp.zeros((ROWS, W), BF16)
    copies = []
    for q in range(NDOM):
        buf[q] = xs[jnp.where(send_live[0, q] > 0, send_block[0, q], NB)]
        if q % PART == PART - 1:
            part = pl.ds(q + 1 - PART, PART)
            copies.append(pltpu.make_async_copy(buf.at[part], out.at[part], sems.at[q // PART]))
            copies[-1].start()
    for copy in copies:
        copy.wait()


def local_fwd_kernel(
    live, first, coord, rem_dst, send_block, send_live, feats, weight, bias, vals, rem, cot,
    local, xs, w_here, wt_here, bias_here, rem_here, cot_here, places, rem_t, vals_t, vals_here, rem_buf, vals_buf, sems,
):
    copies = [
        pltpu.make_async_copy(vals, vals_here, sems.at[0]),
        pltpu.make_async_copy(rem, rem_here, sems.at[1]),
        pltpu.make_async_copy(cot, cot_here, sems.at[2]),
    ]
    for copy in copies:
        copy.start()
    for c in range(NCOL):
        for t in range(2):
            r = (2 * c + t) * ROWS
            w_here[r : r + ROWS] = weight[t, c * ROWS : (c + 1) * ROWS]
    wt_here[...] = w_here[...].astype(F32).T.astype(BF16)
    bias_here[...] = jnp.broadcast_to(bias[...], (W, H)).T
    for b in range(NB):
        xs[b] = masked_block(feats, live[0], b)
    local[...] = jnp.zeros_like(local)
    for q in range(NDOM):
        places[0, q] = rem_dst[0, q]
        places[1, q] = jnp.where(send_live[0, q] > 0, send_block[0, q], NB)
    places[4, 0] = first[0]
    for k in range(LOC):
        places[2, k] = coord[0, k]
        places[3, k] = coord[1, k]
    copies[0].wait()
    for k in range(LOC):
        local[coord[1, k]] += dot(xs[coord[0, k]], vals_here[k])
    for k in range(LOC):
        vals_buf[k] = vals_here[k].T
    copies[1].wait()
    copies.append(pltpu.make_async_copy(vals_buf, vals_t, sems.at[3]))
    copies[-1].start()
    for i in range(NDOM // PART):
        part = pl.ds(i * PART, PART)
        for q in range(i * PART, (i + 1) * PART):
            rem_buf[q] = rem_here[q].T
        copies.append(pltpu.make_async_copy(rem_buf.at[part], rem_t.at[part], sems.at[4 + i]))
        copies[-1].start()
    for copy in copies[2:]:
        copy.wait()


def agg_kernel(live, places, xs, arrived, local, rem, out, *accs):
    accs[0][...] = local[...]
    for acc in accs[1:]:
        acc[...] = jnp.zeros_like(acc)
    for q in range(NDOM):
        accs[q % WAYS][places[0, q]] += dot(arrived[q], rem[q])
    for c in range(NCOL):
        for j in range(2):
            b = 2 * c + j
            out[c, 0:ROWS, j * W : (j + 1) * W] = xs[b]
            out[c, ROWS : 2 * ROWS, j * W : (j + 1) * W] = (add_up(accs, b) * node_mask(live[0], b)).astype(BF16)


def dense_kernel(live, places, got, wt, w, bias, cot, hidden, out):
    node = lax.broadcasted_iota(jnp.int32, (H, H), 1) + places[4, 0]
    mask = (node < live[0]).astype(F32)
    x = got[...].reshape(NCOL * 2 * ROWS, H)
    z = dot(wt[...], x) + jnp.concatenate([bias[...], bias[...]], axis=1)
    sig = 1.0 / (1.0 + jnp.exp(-z))
    hidden[...] = (z * sig * mask).astype(BF16)
    dz = (cot[...].astype(F32) * (sig * (1.0 + z * (1.0 - sig))) * mask).astype(BF16)
    dx = dot(w[...], dz)
    dw = dot(x, dz, NT)
    db = dot(jnp.ones((ROWS, H), BF16), dz, NT)
    mask_rows = mask[0:ROWS]
    row = lax.broadcasted_iota(jnp.int32, (8, W), 0)
    db = jnp.where(row == 0, db[0:8, 0:W], db[0:8, W : 2 * W]).astype(BF16)
    for c in range(NCOL):
        r = c * 2 * ROWS
        direct = dx[r : r + ROWS].astype(BF16)
        dagg = (dx[r + ROWS : r + 2 * ROWS] * mask_rows).astype(BF16)
        for j in range(2):
            lanes = slice(j * W, (j + 1) * W)
            out[c, DIRECT + j * ROWS : DIRECT + (j + 1) * ROWS] = direct[:, lanes]
            out[c, DAGG + j * ROWS : DAGG + (j + 1) * ROWS] = dagg[:, lanes]
            for t in range(2):
                i = DWS + (2 * t + j) * ROWS
                out[c, i : i + ROWS] = dw[r + t * ROWS : r + (t + 1) * ROWS, lanes].astype(BF16)
        out[c, DBS:DBS + 8] = db


def load_grad_blocks(got, gs):
    for c in range(NCOL):
        for j in range(2):
            gs[2 * c + j] = got[c, DAGG + j * ROWS : DAGG + (j + 1) * ROWS]


def add_sums(got, start, middle, end, count):
    dw = got[0, start:middle].astype(F32)
    db = got[0, middle:end].astype(F32)
    for i in range(1, count):
        dw = dw + got[i, start:middle].astype(F32)
        db = db + got[i, middle:end].astype(F32)
    return dw, db


def back_kernel(places, got, rem, vals, hidden, out, local, hidden_out, gs, sem, *accs):
    copy = pltpu.make_async_copy(hidden, hidden_out, sem)
    copy.start()

    @pl.when(places[0, 0] >= 0)
    def _():
        back_body(places, got, rem, vals, out, local, gs, accs)

    copy.wait()


def back_body(places, got, rem, vals, out, local, gs, accs):
    load_grad_blocks(got, gs)
    for c in range(NCOL):
        for j in range(2):
            accs[0][2 * c + j] = got[c, DIRECT + j * ROWS : DIRECT + (j + 1) * ROWS].astype(F32)
    for acc in accs[1:]:
        acc[...] = jnp.zeros_like(acc)
    dw, db = add_sums(got, DWS, DBS, DBS + 8, NCOL)
    for z in range(NZ):
        out[z, DW:DB] = dw.astype(BF16)
        out[z, DB:TALL] = db.astype(BF16)
    for q in range(NDOM):
        x, z, core = q // (NZ * NCORE), q // NCORE % NZ, q % NCORE
        g = x * NCORE + core
        out[z, g * ROWS : (g + 1) * ROWS] = dot(gs[places[0, q]], rem[q]).astype(BF16)
    for k in range(LOC):
        accs[k % WAYS][places[2, k]] += dot(gs[places[3, k]], vals[k])
    for b in range(NB):
        local[b] = add_up(accs, b)


def turn_kernel(got, out):
    for g in range(G):
        for z in range(NZ):
            out[g, z * ROWS : (z + 1) * ROWS] = got[z, g * ROWS : (g + 1) * ROWS]
    dw, db = add_sums(got, DW, DB, TALL, NZ)
    for g in range(G):
        out[g, DW:DB] = dw.astype(BF16)
        out[g, DB:TALL] = db.astype(BF16)


def final_kernel(factor, live, places, local, got, grad, gw, gb, *accs):
    accs[0][0:NB] = local[...]
    for acc in accs[1:]:
        acc[...] = jnp.zeros_like(acc)
    for q in range(NDOM):
        x, z, core = q // (NZ * NCORE), q // NCORE % NZ, q % NCORE
        g = x * NCORE + core
        accs[q % WAYS][places[1, q]] += got[g, z * ROWS : (z + 1) * ROWS].astype(F32)
    for b in range(NB):
        grad[:, b * W : (b + 1) * W] = add_up(accs, b) * node_mask(live[0], b)
    dw, db = add_sums(got, DW, DB, TALL, G)
    dw = dw * factor
    for t in range(2):
        for h in range(2):
            r = (2 * t + h) * ROWS
            gw[t, :, h * W : (h + 1) * W] = dw[r : r + ROWS]
    gb[...] = db[0:2] * factor


def shards(
    feats,
    part_len,
    loc_vals,
    loc_coord,
    send_block,
    send_live,
    rem_vals,
    rem_dst,
    weight,
    bias,
    cot,
):
    sds = jax.ShapeDtypeStruct
    slots = feats.shape[1]
    first = (lax.axis_index("col") * (slots // NCOL)).astype(jnp.int32).reshape(1)
    factor = 1.0 / float(slots * NDOM) ** 0.5
    at = lambda x, z, core: (x * NZ + z) * NCORE + core
    over_xcore = [[at(x, z, core) for x in range(NX) for core in range(NCORE)] for z in range(NZ)]
    over_z = [[at(x, z, core) for z in range(NZ)] for x in range(NX) for core in range(NCORE)]

    def swap(x, axis, groups=None):
        return lax.all_to_all(x, axis, split_axis=0, concat_axis=0, tiled=True, axis_index_groups=groups)

    picked = call(
        pick_kernel,
        pltpu.HBM((NDOM, ROWS, W), BF16),
        [SMEM, SMEM, SMEM, VMEM],
        [
            pltpu.VMEM((NB + 1, ROWS, W), BF16),
            pltpu.VMEM((NDOM, ROWS, W), BF16),
            pltpu.SemaphoreType.DMA((NDOM // PART,)),
        ],
        nbytes=320 * 1024,
        name="pick",
    )(part_len, in_hbm(send_block), in_hbm(send_live), in_hbm(feats))
    arrived = swap(picked.reshape(NDOM, 2, 8, W), "dom").reshape(NDOM, ROWS, W)
    local, xs, w_here, wt_here, bias_here, rem_here, cot_here, places, rem_t, vals_t = call(
        local_fwd_kernel,
        [
            pltpu.VMEM((NB, ROWS, W), F32),
            pltpu.VMEM((NB, ROWS, W), BF16),
            pltpu.VMEM((H, H), BF16),
            pltpu.VMEM((H, H), BF16),
            pltpu.VMEM((H, W), F32),
            pltpu.VMEM(rem_vals.shape, BF16),
            pltpu.VMEM(cot.shape, BF16),
            pltpu.SMEM((5, NDOM), jnp.int32),
            pltpu.HBM(rem_vals.shape, BF16),
            pltpu.HBM(loc_vals.shape, BF16),
        ],
        [SMEM] * 6 + [VMEM] * 3 + [ANY] * 3,
        [
            pltpu.VMEM((LOC, W, W), BF16),
            pltpu.VMEM((NDOM, W, W), BF16),
            pltpu.VMEM((LOC, W, W), BF16),
            pltpu.SemaphoreType.DMA((4 + NDOM // PART,)),
        ],
        flops=2 * LOC * ROWS * W * W,
        nbytes=4 * 2**20,
        name="local_fwd",
    )(
        part_len,
        first,
        in_hbm(loc_coord.T),
        in_hbm(rem_dst),
        in_hbm(send_block),
        in_hbm(send_live),
        in_hbm(feats),
        in_hbm(weight),
        in_hbm(bias.reshape(1, H)),
        in_hbm(loc_vals),
        in_hbm(rem_vals),
        in_hbm(cot),
    )
    stacked = call(
        agg_kernel,
        pltpu.VMEM((NCOL, 2 * ROWS, 2 * W), BF16),
        [SMEM, SMEM] + [VMEM] * 4,
        [pltpu.VMEM((NB, ROWS, W), F32)] * WAYS,
        flops=2 * NDOM * ROWS * W * W,
        nbytes=3 * 2**20,
        name="agg",
    )(part_len, places, in_vmem(xs), in_vmem(arrived), in_vmem(local), in_vmem(rem_here))
    regrouped = swap(stacked, "col")
    hidden_here, outgoing = call(
        dense_kernel,
        [pltpu.VMEM((H, 2 * W), BF16), pltpu.VMEM((NCOL, HIGH, W), BF16)],
        [SMEM, SMEM] + [VMEM] * 5,
        flops=3 * 2 * H**3,
        nbytes=2**20,
        name="dense",
    )(part_len, places, in_vmem(regrouped), in_vmem(wt_here), in_vmem(w_here), in_vmem(bias_here), in_vmem(cot_here))
    returned = swap(outgoing.reshape(NCOL, HIGH // 8, 8, W), "col").reshape(NCOL, HIGH, W)
    terms, local_back, hidden = call(
        back_kernel,
        [pltpu.VMEM((NZ, TALL, W), BF16), pltpu.VMEM((NB, ROWS, W), F32), pltpu.HBM((H, 2 * W), BF16)],
        [SMEM, VMEM, VMEM, VMEM, ANY],
        [pltpu.VMEM((NB, ROWS, W), BF16), pltpu.SemaphoreType.DMA] + [pltpu.VMEM((NB, ROWS, W), F32)] * WAYS,
        flops=2 * (NDOM + LOC) * ROWS * W * W,
        nbytes=4 * 2**20,
        name="back",
    )(places, in_vmem(returned), in_vmem(rem_t), in_vmem(vals_t), in_vmem(hidden_here))
    half = swap(terms.reshape(NZ, TALL // 8, 8, W), "dom", over_z).reshape(NZ, TALL, W)
    turned = call(
        turn_kernel,
        pltpu.VMEM((G, TALL, W), BF16),
        [VMEM],
        nbytes=2**20,
        name="turn",
    )(in_vmem(half))
    got = swap(turned.reshape(G, TALL // 8, 8, W), "dom", over_xcore).reshape(G, TALL, W)

    def final_body(*refs):
        final_kernel(factor, *refs)

    grad_feats, grad_weight, grad_bias = call(
        final_body,
        [sds((ROWS, slots), F32), sds((2, ROWS, H), F32), sds((2, W), F32)],
        [SMEM, SMEM, VMEM, VMEM],
        [pltpu.VMEM((NB + 1, ROWS, W), F32)] * WAYS,
        nbytes=2**20,
        name="final",
    )(part_len, places, in_vmem(local_back), in_vmem(got))
    return (hidden, grad_feats, grad_weight, grad_bias.reshape(H))


def solution(mesh):
    placed = (
        P("col", "dom"),
        P("dom"),
        P("dom", None, None),
        P("dom", None),
        P("dom", None),
        P("dom", None),
        P("dom", None, None),
        P("dom", None),
        P(),
        P(),
        P(None, ("dom", "col")),
    )
    return jax.shard_map(
        shards,
        mesh=mesh,
        in_specs=placed,
        out_specs=(P(None, ("dom", "col")), P("col", "dom"), P(None, "col", None), P()),
        check_vma=False,
    )
```

```python
import jax
import jax.numpy as jnp
from jax import lax
from jax.experimental import pallas as pl
from jax.experimental.pallas import tpu as pltpu
from jax.sharding import PartitionSpec as P

F32 = jnp.float32
BF16 = jnp.bfloat16
NX, NZ, NCORE = 4, 8, 2
NDOM = NX * NZ * NCORE
NCOL = 8
NB = 16
W = 128
ROWS = 16
H = 256
LOC = 24
WAYS = 2
PART = 16
G = NX * NCORE
DW = NZ * ROWS
DB = DW + 4 * ROWS
TALL = DB + 8
DIRECT, DAGG, DWS, DBS = 0, 2 * ROWS, 4 * ROWS, 8 * ROWS
HIGH = DBS + 16

SMEM = pl.BlockSpec(memory_space=pltpu.SMEM)
VMEM = pl.BlockSpec(memory_space=pltpu.VMEM)
ANY = pl.BlockSpec(memory_space=pl.ANY)
NT = (((1,), (1,)), ((), ()))
NN = (((1,), (0,)), ((), ()))


def dot(a, b, dims=NN):
    return lax.dot_general(a, b, dims, preferred_element_type=F32)


def call(body, out_shape, in_specs, scratch=(), flops=0, nbytes=0, name=None):
    many = isinstance(out_shape, (list, tuple))
    return pl.pallas_call(
        body,
        out_shape=out_shape,
        in_specs=in_specs,
        out_specs=[out_spec(s) for s in out_shape] if many else out_spec(out_shape),
        scratch_shapes=list(scratch),
        compiler_params=pltpu.CompilerParams(vmem_limit_bytes=8 * 2**20),
        cost_estimate=pl.CostEstimate(flops=flops, bytes_accessed=nbytes, transcendentals=0),
        name=name,
    )


def out_spec(shape):
    return {pltpu.SMEM: SMEM, pltpu.HBM: ANY}.get(getattr(shape, "memory_space", None), VMEM)


def in_hbm(x):
    return pltpu.with_memory_space_constraint(x, pltpu.HBM)


def in_vmem(x):
    return pltpu.with_memory_space_constraint(x, pltpu.VMEM)


def masked_block(feats, live, b):
    node = lax.broadcasted_iota(jnp.int32, (ROWS, W), 1) + b * W
    return jnp.where(node < live, feats[:, b * W : (b + 1) * W].astype(F32), 0.0).astype(BF16)


def node_mask(live, b):
    node = lax.broadcasted_iota(jnp.int32, (ROWS, W), 1) + b * W
    return (node < live).astype(F32)


def add_up(accs, b):
    total = accs[0][b]
    for acc in accs[1:]:
        total = total + acc[b]
    return total


def pick_kernel(live, send_block, send_live, feats, out, xs, buf, sems):
    for b in range(NB):
        xs[b] = masked_block(feats, live[0], b)
    xs[NB] = jnp.zeros((ROWS, W), BF16)
    copies = []
    for q in range(NDOM):
        buf[q] = xs[jnp.where(send_live[0, q] > 0, send_block[0, q], NB)]
        if q % PART == PART - 1:
            part = pl.ds(q + 1 - PART, PART)
            copies.append(pltpu.make_async_copy(buf.at[part], out.at[part], sems.at[q // PART]))
            copies[-1].start()
    for copy in copies:
        copy.wait()


def local_fwd_kernel(
    live, first, coord, rem_dst, send_block, send_live, feats, weight, bias, vals, rem, cot,
    local, xs, w_here, wt_here, bias_here, rem_here, cot_here, places, rem_t, vals_t, vals_here, rem_buf, vals_buf, sems,
):
    copies = [
        pltpu.make_async_copy(vals, vals_here, sems.at[0]),
        pltpu.make_async_copy(rem, rem_here, sems.at[1]),
        pltpu.make_async_copy(cot, cot_here, sems.at[2]),
    ]
    for copy in copies:
        copy.start()
    for c in range(NCOL):
        for t in range(2):
            r = (2 * c + t) * ROWS
            w_here[r : r + ROWS] = weight[t, c * ROWS : (c + 1) * ROWS]
    wt_here[...] = w_here[...].astype(F32).T.astype(BF16)
    bias_here[...] = jnp.broadcast_to(bias[...], (W, H)).T
    for b in range(NB):
        xs[b] = masked_block(feats, live[0], b)
    local[...] = jnp.zeros_like(local)
    for q in range(NDOM):
        places[0, q] = rem_dst[0, q]
        places[1, q] = jnp.where(send_live[0, q] > 0, send_block[0, q], NB)
    places[4, 0] = first[0]
    for k in range(LOC):
        places[2, k] = coord[0, k]
        places[3, k] = coord[1, k]
    copies[0].wait()
    for k in range(LOC):
        local[coord[1, k]] += dot(xs[coord[0, k]], vals_here[k])
    for k in range(LOC):
        vals_buf[k] = vals_here[k].T
    copies[1].wait()
    copies.append(pltpu.make_async_copy(vals_buf, vals_t, sems.at[3]))
    copies[-1].start()
    for i in range(NDOM // PART):
        part = pl.ds(i * PART, PART)
        for q in range(i * PART, (i + 1) * PART):
            rem_buf[q] = rem_here[q].T
        copies.append(pltpu.make_async_copy(rem_buf.at[part], rem_t.at[part], sems.at[4 + i]))
        copies[-1].start()
    for copy in copies[2:]:
        copy.wait()


def agg_kernel(live, places, xs, arrived, local, rem, out, *accs):
    accs[0][...] = local[...]
    for acc in accs[1:]:
        acc[...] = jnp.zeros_like(acc)
    for q in range(NDOM):
        accs[q % WAYS][places[0, q]] += dot(arrived[q], rem[q])
    for c in range(NCOL):
        for j in range(2):
            b = 2 * c + j
            out[c, 0:ROWS, j * W : (j + 1) * W] = xs[b]
            out[c, ROWS : 2 * ROWS, j * W : (j + 1) * W] = (add_up(accs, b) * node_mask(live[0], b)).astype(BF16)


def dense_kernel(live, places, got, wt, w, bias, cot, hidden, out):
    node = lax.broadcasted_iota(jnp.int32, (H, H), 1) + places[4, 0]
    mask = (node < live[0]).astype(F32)
    x = got[...].reshape(NCOL * 2 * ROWS, H)
    z = dot(wt[...], x) + jnp.concatenate([bias[...], bias[...]], axis=1)
    sig = 1.0 / (1.0 + jnp.exp(-z))
    hidden[...] = (z * sig * mask).astype(BF16)
    dz = (cot[...].astype(F32) * (sig * (1.0 + z * (1.0 - sig))) * mask).astype(BF16)
    dx = dot(w[...], dz)
    dw = dot(x, dz, NT)
    db = dot(jnp.ones((ROWS, H), BF16), dz, NT)
    mask_rows = mask[0:ROWS]
    row = lax.broadcasted_iota(jnp.int32, (8, W), 0)
    db = jnp.where(row == 0, db[0:8, 0:W], db[0:8, W : 2 * W]).astype(BF16)
    for c in range(NCOL):
        r = c * 2 * ROWS
        direct = dx[r : r + ROWS].astype(BF16)
        dagg = (dx[r + ROWS : r + 2 * ROWS] * mask_rows).astype(BF16)
        for j in range(2):
            lanes = slice(j * W, (j + 1) * W)
            out[c, DIRECT + j * ROWS : DIRECT + (j + 1) * ROWS] = direct[:, lanes]
            out[c, DAGG + j * ROWS : DAGG + (j + 1) * ROWS] = dagg[:, lanes]
            for t in range(2):
                i = DWS + (2 * t + j) * ROWS
                out[c, i : i + ROWS] = dw[r + t * ROWS : r + (t + 1) * ROWS, lanes].astype(BF16)
        out[c, DBS:DBS + 8] = db


def load_grad_blocks(got, gs):
    for c in range(NCOL):
        for j in range(2):
            gs[2 * c + j] = got[c, DAGG + j * ROWS : DAGG + (j + 1) * ROWS]


def add_sums(got, start, middle, end, count):
    dw = got[0, start:middle].astype(F32)
    db = got[0, middle:end].astype(F32)
    for i in range(1, count):
        dw = dw + got[i, start:middle].astype(F32)
        db = db + got[i, middle:end].astype(F32)
    return dw, db


def back_kernel(places, got, rem, vals, hidden, out, local, hidden_out, gs, sem, *accs):
    copy = pltpu.make_async_copy(hidden, hidden_out, sem)
    copy.start()

    @pl.when(places[0, 0] >= 0)
    def _():
        back_body(places, got, rem, vals, out, local, gs, accs)

    copy.wait()


def back_body(places, got, rem, vals, out, local, gs, accs):
    load_grad_blocks(got, gs)
    for c in range(NCOL):
        for j in range(2):
            accs[0][2 * c + j] = got[c, DIRECT + j * ROWS : DIRECT + (j + 1) * ROWS].astype(F32)
    for acc in accs[1:]:
        acc[...] = jnp.zeros_like(acc)
    dw, db = add_sums(got, DWS, DBS, DBS + 8, NCOL)
    for z in range(NZ):
        out[z, DW:DB] = dw.astype(BF16)
        out[z, DB:TALL] = db.astype(BF16)
    for q in range(NDOM):
        x, z, core = q // (NZ * NCORE), q // NCORE % NZ, q % NCORE
        g = x * NCORE + core
        out[z, g * ROWS : (g + 1) * ROWS] = dot(gs[places[0, q]], rem[q]).astype(BF16)
    for k in range(LOC):
        accs[k % WAYS][places[2, k]] += dot(gs[places[3, k]], vals[k])
    for b in range(NB):
        local[b] = add_up(accs, b)


def turn_kernel(got, out):
    for g in range(G):
        for z in range(NZ):
            out[g, z * ROWS : (z + 1) * ROWS] = got[z, g * ROWS : (g + 1) * ROWS]
    dw, db = add_sums(got, DW, DB, TALL, NZ)
    for g in range(G):
        out[g, DW:DB] = dw.astype(BF16)
        out[g, DB:TALL] = db.astype(BF16)


def final_kernel(factor, live, places, local, got, grad, gw, gb, *accs):
    accs[0][0:NB] = local[...]
    for acc in accs[1:]:
        acc[...] = jnp.zeros_like(acc)
    for q in range(NDOM):
        x, z, core = q // (NZ * NCORE), q // NCORE % NZ, q % NCORE
        g = x * NCORE + core
        accs[q % WAYS][places[1, q]] += got[g, z * ROWS : (z + 1) * ROWS].astype(F32)
    for b in range(NB):
        grad[:, b * W : (b + 1) * W] = add_up(accs, b) * node_mask(live[0], b)
    dw, db = add_sums(got, DW, DB, TALL, G)
    dw = dw * factor
    for t in range(2):
        for h in range(2):
            r = (2 * t + h) * ROWS
            gw[t, :, h * W : (h + 1) * W] = dw[r : r + ROWS]
    gb[...] = db[0:2] * factor


def shards(
    feats,
    part_len,
    loc_vals,
    loc_coord,
    send_block,
    send_live,
    rem_vals,
    rem_dst,
    weight,
    bias,
    cot,
):
    sds = jax.ShapeDtypeStruct
    slots = feats.shape[1]
    first = (lax.axis_index("col") * (slots // NCOL)).astype(jnp.int32).reshape(1)
    factor = 1.0 / float(slots * NDOM) ** 0.5
    at = lambda x, z, core: (x * NZ + z) * NCORE + core
    over_xcore = [[at(x, z, core) for x in range(NX) for core in range(NCORE)] for z in range(NZ)]
    over_z = [[at(x, z, core) for z in range(NZ)] for x in range(NX) for core in range(NCORE)]

    def swap(x, axis, groups=None):
        return lax.all_to_all(x, axis, split_axis=0, concat_axis=0, tiled=True, axis_index_groups=groups)

    picked = call(
        pick_kernel,
        pltpu.HBM((NDOM, ROWS, W), BF16),
        [SMEM, SMEM, SMEM, VMEM],
        [
            pltpu.VMEM((NB + 1, ROWS, W), BF16),
            pltpu.VMEM((NDOM, ROWS, W), BF16),
            pltpu.SemaphoreType.DMA((NDOM // PART,)),
        ],
        nbytes=320 * 1024,
        name="pick",
    )(part_len, in_hbm(send_block), in_hbm(send_live), in_hbm(feats))
    arrived = swap(picked, "dom")
    local, xs, w_here, wt_here, bias_here, rem_here, cot_here, places, rem_t, vals_t = call(
        local_fwd_kernel,
        [
            pltpu.VMEM((NB, ROWS, W), F32),
            pltpu.VMEM((NB, ROWS, W), BF16),
            pltpu.VMEM((H, H), BF16),
            pltpu.VMEM((H, H), BF16),
            pltpu.VMEM((H, W), F32),
            pltpu.VMEM(rem_vals.shape, BF16),
            pltpu.VMEM(cot.shape, BF16),
            pltpu.SMEM((5, NDOM), jnp.int32),
            pltpu.HBM(rem_vals.shape, BF16),
            pltpu.HBM(loc_vals.shape, BF16),
        ],
        [SMEM] * 6 + [VMEM] * 3 + [ANY] * 3,
        [
            pltpu.VMEM((LOC, W, W), BF16),
            pltpu.VMEM((NDOM, W, W), BF16),
            pltpu.VMEM((LOC, W, W), BF16),
            pltpu.SemaphoreType.DMA((4 + NDOM // PART,)),
        ],
        flops=2 * LOC * ROWS * W * W,
        nbytes=4 * 2**20,
        name="local_fwd",
    )(
        part_len,
        first,
        in_hbm(loc_coord.T),
        in_hbm(rem_dst),
        in_hbm(send_block),
        in_hbm(send_live),
        in_hbm(feats),
        in_hbm(weight),
        in_hbm(bias.reshape(1, H)),
        in_hbm(loc_vals),
        in_hbm(rem_vals),
        in_hbm(cot),
    )
    stacked = call(
        agg_kernel,
        pltpu.VMEM((NCOL, 2 * ROWS, 2 * W), BF16),
        [SMEM, SMEM] + [VMEM] * 4,
        [pltpu.VMEM((NB, ROWS, W), F32)] * WAYS,
        flops=2 * NDOM * ROWS * W * W,
        nbytes=3 * 2**20,
        name="agg",
    )(part_len, places, in_vmem(xs), in_vmem(arrived), in_vmem(local), in_vmem(rem_here))
    regrouped = swap(stacked, "col")
    hidden_here, outgoing = call(
        dense_kernel,
        [pltpu.VMEM((H, 2 * W), BF16), pltpu.VMEM((NCOL, HIGH, W), BF16)],
        [SMEM, SMEM] + [VMEM] * 5,
        flops=3 * 2 * H**3,
        nbytes=2**20,
        name="dense",
    )(part_len, places, in_vmem(regrouped), in_vmem(wt_here), in_vmem(w_here), in_vmem(bias_here), in_vmem(cot_here))
    returned = swap(outgoing, "col")
    terms, local_back, hidden = call(
        back_kernel,
        [pltpu.VMEM((NZ, TALL, W), BF16), pltpu.VMEM((NB, ROWS, W), F32), pltpu.HBM((H, 2 * W), BF16)],
        [SMEM, VMEM, VMEM, VMEM, ANY],
        [pltpu.VMEM((NB, ROWS, W), BF16), pltpu.SemaphoreType.DMA] + [pltpu.VMEM((NB, ROWS, W), F32)] * WAYS,
        flops=2 * (NDOM + LOC) * ROWS * W * W,
        nbytes=4 * 2**20,
        name="back",
    )(places, in_vmem(returned), in_vmem(rem_t), in_vmem(vals_t), in_vmem(hidden_here))
    half = swap(terms, "dom", over_z)
    turned = call(
        turn_kernel,
        pltpu.VMEM((G, TALL, W), BF16),
        [VMEM],
        nbytes=2**20,
        name="turn",
    )(in_vmem(half))
    got = swap(turned, "dom", over_xcore)

    def final_body(*refs):
        final_kernel(factor, *refs)

    grad_feats, grad_weight, grad_bias = call(
        final_body,
        [sds((ROWS, slots), F32), sds((2, ROWS, H), F32), sds((2, W), F32)],
        [SMEM, SMEM, VMEM, VMEM],
        [pltpu.VMEM((NB + 1, ROWS, W), F32)] * WAYS,
        nbytes=2**20,
        name="final",
    )(part_len, places, in_vmem(local_back), in_vmem(got))
    return (hidden, grad_feats, grad_weight, grad_bias.reshape(H))


def solution(mesh):
    placed = (
        P("col", "dom"),
        P("dom"),
        P("dom", None, None),
        P("dom", None),
        P("dom", None),
        P("dom", None),
        P("dom", None, None),
        P("dom", None),
        P(),
        P(),
        P(None, ("dom", "col")),
    )
    return jax.shard_map(
        shards,
        mesh=mesh,
        in_specs=placed,
        out_specs=(P(None, ("dom", "col")), P("col", "dom"), P(None, "col", None), P()),
        check_vma=False,
    )
```

```python
import jax
import jax.numpy as jnp
from jax import lax
from jax.experimental import pallas as pl
from jax.experimental.pallas import tpu as pltpu
from jax.sharding import PartitionSpec as P

F32 = jnp.float32
BF16 = jnp.bfloat16
NX, NZ, NCORE = 4, 8, 2
NDOM = NX * NZ * NCORE
NCOL = 8
NB = 16
W = 128
ROWS = 16
H = 256
LOC = 24
WAYS = 4
PART = 32
G = NX * NCORE
DW = NZ * ROWS
DB = DW + 4 * ROWS
TALL = DB + 8
DIRECT, DAGG, DWS, DBS = 0, 2 * ROWS, 4 * ROWS, 8 * ROWS
HIGH = DBS + 16

SMEM = pl.BlockSpec(memory_space=pltpu.SMEM)
VMEM = pl.BlockSpec(memory_space=pltpu.VMEM)
ANY = pl.BlockSpec(memory_space=pl.ANY)
NT = (((1,), (1,)), ((), ()))
NN = (((1,), (0,)), ((), ()))


def dot(a, b, dims=NN):
    return lax.dot_general(a, b, dims, preferred_element_type=F32)


def call(body, out_shape, in_specs, scratch=(), flops=0, nbytes=0, name=None):
    many = isinstance(out_shape, (list, tuple))
    return pl.pallas_call(
        body,
        out_shape=out_shape,
        in_specs=in_specs,
        out_specs=[out_spec(s) for s in out_shape] if many else out_spec(out_shape),
        scratch_shapes=list(scratch),
        compiler_params=pltpu.CompilerParams(vmem_limit_bytes=8 * 2**20),
        cost_estimate=pl.CostEstimate(flops=flops, bytes_accessed=nbytes, transcendentals=0),
        name=name,
    )


def out_spec(shape):
    return {pltpu.SMEM: SMEM, pltpu.HBM: ANY}.get(getattr(shape, "memory_space", None), VMEM)


def in_hbm(x):
    return pltpu.with_memory_space_constraint(x, pltpu.HBM)


def in_vmem(x):
    return pltpu.with_memory_space_constraint(x, pltpu.VMEM)


def masked_block(feats, live, b):
    node = lax.broadcasted_iota(jnp.int32, (ROWS, W), 1) + b * W
    return jnp.where(node < live, feats[:, b * W : (b + 1) * W].astype(F32), 0.0).astype(BF16)


def node_mask(live, b):
    node = lax.broadcasted_iota(jnp.int32, (ROWS, W), 1) + b * W
    return (node < live).astype(F32)


def add_up(accs, b):
    total = accs[0][b]
    for acc in accs[1:]:
        total = total + acc[b]
    return total


def pick_kernel(live, send_block, send_live, feats, out, xs, buf, sems):
    for b in range(NB):
        xs[b] = masked_block(feats, live[0], b)
    xs[NB] = jnp.zeros((ROWS, W), BF16)
    copies = []
    for q in range(NDOM):
        buf[q] = xs[jnp.where(send_live[0, q] > 0, send_block[0, q], NB)]
        if q % PART == PART - 1:
            part = pl.ds(q + 1 - PART, PART)
            copies.append(pltpu.make_async_copy(buf.at[part], out.at[part], sems.at[q // PART]))
            copies[-1].start()
    for copy in copies:
        copy.wait()


def local_fwd_kernel(
    live, first, coord, rem_dst, send_block, send_live, feats, weight, bias, vals, rem, cot,
    local, xs, w_here, wt_here, bias_here, rem_here, cot_here, places, rem_t, vals_t, vals_here, rem_buf, vals_buf, sems,
):
    copies = [
        pltpu.make_async_copy(vals, vals_here, sems.at[0]),
        pltpu.make_async_copy(rem, rem_here, sems.at[1]),
        pltpu.make_async_copy(cot, cot_here, sems.at[2]),
    ]
    for copy in copies:
        copy.start()
    for c in range(NCOL):
        for t in range(2):
            r = (2 * c + t) * ROWS
            w_here[r : r + ROWS] = weight[t, c * ROWS : (c + 1) * ROWS]
    wt_here[...] = w_here[...].astype(F32).T.astype(BF16)
    bias_here[...] = jnp.broadcast_to(bias[...], (W, H)).T
    for b in range(NB):
        xs[b] = masked_block(feats, live[0], b)
    local[...] = jnp.zeros_like(local)
    for q in range(NDOM):
        places[0, q] = rem_dst[0, q]
        places[1, q] = jnp.where(send_live[0, q] > 0, send_block[0, q], NB)
    places[4, 0] = first[0]
    for k in range(LOC):
        places[2, k] = coord[0, k]
        places[3, k] = coord[1, k]
    copies[0].wait()
    for k in range(LOC):
        local[coord[1, k]] += dot(xs[coord[0, k]], vals_here[k])
    for k in range(LOC):
        vals_buf[k] = vals_here[k].T
    copies[1].wait()
    copies.append(pltpu.make_async_copy(vals_buf, vals_t, sems.at[3]))
    copies[-1].start()
    for i in range(NDOM // PART):
        part = pl.ds(i * PART, PART)
        for q in range(i * PART, (i + 1) * PART):
            rem_buf[q] = rem_here[q].T
        copies.append(pltpu.make_async_copy(rem_buf.at[part], rem_t.at[part], sems.at[4 + i]))
        copies[-1].start()
    for copy in copies[2:]:
        copy.wait()


def agg_kernel(live, places, xs, arrived, local, rem, out, *accs):
    accs[0][...] = local[...]
    for acc in accs[1:]:
        acc[...] = jnp.zeros_like(acc)
    for q in range(NDOM):
        accs[q % WAYS][places[0, q]] += dot(arrived[q], rem[q])
    for c in range(NCOL):
        for j in range(2):
            b = 2 * c + j
            out[c, 0:ROWS, j * W : (j + 1) * W] = xs[b]
            out[c, ROWS : 2 * ROWS, j * W : (j + 1) * W] = (add_up(accs, b) * node_mask(live[0], b)).astype(BF16)


def dense_kernel(live, places, got, wt, w, bias, cot, hidden, out):
    node = lax.broadcasted_iota(jnp.int32, (H, H), 1) + places[4, 0]
    mask = (node < live[0]).astype(F32)
    x = got[...].reshape(NCOL * 2 * ROWS, H)
    z = dot(wt[...], x) + jnp.concatenate([bias[...], bias[...]], axis=1)
    sig = 1.0 / (1.0 + jnp.exp(-z))
    hidden[...] = (z * sig * mask).astype(BF16)
    dz = (cot[...].astype(F32) * (sig * (1.0 + z * (1.0 - sig))) * mask).astype(BF16)
    dx = dot(w[...], dz)
    dw = dot(x, dz, NT)
    db = dot(jnp.ones((ROWS, H), BF16), dz, NT)
    mask_rows = mask[0:ROWS]
    row = lax.broadcasted_iota(jnp.int32, (8, W), 0)
    db = jnp.where(row == 0, db[0:8, 0:W], db[0:8, W : 2 * W]).astype(BF16)
    for c in range(NCOL):
        r = c * 2 * ROWS
        direct = dx[r : r + ROWS].astype(BF16)
        dagg = (dx[r + ROWS : r + 2 * ROWS] * mask_rows).astype(BF16)
        for j in range(2):
            lanes = slice(j * W, (j + 1) * W)
            out[c, DIRECT + j * ROWS : DIRECT + (j + 1) * ROWS] = direct[:, lanes]
            out[c, DAGG + j * ROWS : DAGG + (j + 1) * ROWS] = dagg[:, lanes]
            for t in range(2):
                i = DWS + (2 * t + j) * ROWS
                out[c, i : i + ROWS] = dw[r + t * ROWS : r + (t + 1) * ROWS, lanes].astype(BF16)
        out[c, DBS:DBS + 8] = db


def load_grad_blocks(got, gs):
    for c in range(NCOL):
        for j in range(2):
            gs[2 * c + j] = got[c, DAGG + j * ROWS : DAGG + (j + 1) * ROWS]


def add_sums(got, start, middle, end, count):
    dw = got[0, start:middle].astype(F32)
    db = got[0, middle:end].astype(F32)
    for i in range(1, count):
        dw = dw + got[i, start:middle].astype(F32)
        db = db + got[i, middle:end].astype(F32)
    return dw, db


def back_kernel(places, got, rem, vals, hidden, out, local, hidden_out, gs, sem, *accs):
    copy = pltpu.make_async_copy(hidden, hidden_out, sem)
    copy.start()

    @pl.when(places[0, 0] >= 0)
    def _():
        back_body(places, got, rem, vals, out, local, gs, accs)

    copy.wait()


def back_body(places, got, rem, vals, out, local, gs, accs):
    load_grad_blocks(got, gs)
    for c in range(NCOL):
        for j in range(2):
            accs[0][2 * c + j] = got[c, DIRECT + j * ROWS : DIRECT + (j + 1) * ROWS].astype(F32)
    for acc in accs[1:]:
        acc[...] = jnp.zeros_like(acc)
    dw, db = add_sums(got, DWS, DBS, DBS + 8, NCOL)
    for z in range(NZ):
        out[z, DW:DB] = dw.astype(BF16)
        out[z, DB:TALL] = db.astype(BF16)
    for q in range(NDOM):
        x, z, core = q // (NZ * NCORE), q // NCORE % NZ, q % NCORE
        g = x * NCORE + core
        out[z, g * ROWS : (g + 1) * ROWS] = dot(gs[places[0, q]], rem[q]).astype(BF16)
    for k in range(LOC):
        accs[k % WAYS][places[2, k]] += dot(gs[places[3, k]], vals[k])
    for b in range(NB):
        local[b] = add_up(accs, b)


def turn_kernel(got, out):
    for g in range(G):
        for z in range(NZ):
            out[g, z * ROWS : (z + 1) * ROWS] = got[z, g * ROWS : (g + 1) * ROWS]
    dw, db = add_sums(got, DW, DB, TALL, NZ)
    for g in range(G):
        out[g, DW:DB] = dw.astype(BF16)
        out[g, DB:TALL] = db.astype(BF16)


def final_kernel(factor, live, places, local, got, grad, gw, gb, *accs):
    accs[0][0:NB] = local[...]
    for acc in accs[1:]:
        acc[...] = jnp.zeros_like(acc)
    for q in range(NDOM):
        x, z, core = q // (NZ * NCORE), q // NCORE % NZ, q % NCORE
        g = x * NCORE + core
        accs[q % WAYS][places[1, q]] += got[g, z * ROWS : (z + 1) * ROWS].astype(F32)
    for b in range(NB):
        grad[:, b * W : (b + 1) * W] = add_up(accs, b) * node_mask(live[0], b)
    dw, db = add_sums(got, DW, DB, TALL, G)
    dw = dw * factor
    for t in range(2):
        for h in range(2):
            r = (2 * t + h) * ROWS
            gw[t, :, h * W : (h + 1) * W] = dw[r : r + ROWS]
    gb[...] = db[0:2] * factor


def shards(
    feats,
    part_len,
    loc_vals,
    loc_coord,
    send_block,
    send_live,
    rem_vals,
    rem_dst,
    weight,
    bias,
    cot,
):
    sds = jax.ShapeDtypeStruct
    slots = feats.shape[1]
    first = (lax.axis_index("col") * (slots // NCOL)).astype(jnp.int32).reshape(1)
    factor = 1.0 / float(slots * NDOM) ** 0.5
    at = lambda x, z, core: (x * NZ + z) * NCORE + core
    over_xcore = [[at(x, z, core) for x in range(NX) for core in range(NCORE)] for z in range(NZ)]
    over_z = [[at(x, z, core) for z in range(NZ)] for x in range(NX) for core in range(NCORE)]

    def swap(x, axis, groups=None):
        return lax.all_to_all(x, axis, split_axis=0, concat_axis=0, tiled=True, axis_index_groups=groups)

    picked = call(
        pick_kernel,
        pltpu.HBM((NDOM, ROWS, W), BF16),
        [SMEM, SMEM, SMEM, VMEM],
        [
            pltpu.VMEM((NB + 1, ROWS, W), BF16),
            pltpu.VMEM((NDOM, ROWS, W), BF16),
            pltpu.SemaphoreType.DMA((NDOM // PART,)),
        ],
        nbytes=320 * 1024,
        name="pick",
    )(part_len, in_hbm(send_block), in_hbm(send_live), in_hbm(feats))
    arrived = swap(picked, "dom")
    local, xs, w_here, wt_here, bias_here, rem_here, cot_here, places, rem_t, vals_t = call(
        local_fwd_kernel,
        [
            pltpu.VMEM((NB, ROWS, W), F32),
            pltpu.VMEM((NB, ROWS, W), BF16),
            pltpu.VMEM((H, H), BF16),
            pltpu.VMEM((H, H), BF16),
            pltpu.VMEM((H, W), F32),
            pltpu.VMEM(rem_vals.shape, BF16),
            pltpu.VMEM(cot.shape, BF16),
            pltpu.SMEM((5, NDOM), jnp.int32),
            pltpu.HBM(rem_vals.shape, BF16),
            pltpu.HBM(loc_vals.shape, BF16),
        ],
        [SMEM] * 6 + [VMEM] * 3 + [ANY] * 3,
        [
            pltpu.VMEM((LOC, W, W), BF16),
            pltpu.VMEM((NDOM, W, W), BF16),
            pltpu.VMEM((LOC, W, W), BF16),
            pltpu.SemaphoreType.DMA((4 + NDOM // PART,)),
        ],
        flops=2 * LOC * ROWS * W * W,
        nbytes=4 * 2**20,
        name="local_fwd",
    )(
        part_len,
        first,
        in_hbm(loc_coord.T),
        in_hbm(rem_dst),
        in_hbm(send_block),
        in_hbm(send_live),
        in_hbm(feats),
        in_hbm(weight),
        in_hbm(bias.reshape(1, H)),
        in_hbm(loc_vals),
        in_hbm(rem_vals),
        in_hbm(cot),
    )
    stacked = call(
        agg_kernel,
        pltpu.VMEM((NCOL, 2 * ROWS, 2 * W), BF16),
        [SMEM, SMEM] + [VMEM] * 4,
        [pltpu.VMEM((NB, ROWS, W), F32)] * WAYS,
        flops=2 * NDOM * ROWS * W * W,
        nbytes=3 * 2**20,
        name="agg",
    )(part_len, places, in_vmem(xs), in_vmem(arrived), in_vmem(local), in_vmem(rem_here))
    regrouped = swap(stacked, "col")
    hidden_here, outgoing = call(
        dense_kernel,
        [pltpu.VMEM((H, 2 * W), BF16), pltpu.VMEM((NCOL, HIGH, W), BF16)],
        [SMEM, SMEM] + [VMEM] * 5,
        flops=3 * 2 * H**3,
        nbytes=2**20,
        name="dense",
    )(part_len, places, in_vmem(regrouped), in_vmem(wt_here), in_vmem(w_here), in_vmem(bias_here), in_vmem(cot_here))
    returned = swap(outgoing, "col")
    terms, local_back, hidden = call(
        back_kernel,
        [pltpu.VMEM((NZ, TALL, W), BF16), pltpu.VMEM((NB, ROWS, W), F32), pltpu.HBM((H, 2 * W), BF16)],
        [SMEM, VMEM, VMEM, VMEM, ANY],
        [pltpu.VMEM((NB, ROWS, W), BF16), pltpu.SemaphoreType.DMA] + [pltpu.VMEM((NB, ROWS, W), F32)] * WAYS,
        flops=2 * (NDOM + LOC) * ROWS * W * W,
        nbytes=4 * 2**20,
        name="back",
    )(places, in_vmem(returned), in_vmem(rem_t), in_vmem(vals_t), in_vmem(hidden_here))
    half = swap(terms, "dom", over_z)
    turned = call(
        turn_kernel,
        pltpu.VMEM((G, TALL, W), BF16),
        [VMEM],
        nbytes=2**20,
        name="turn",
    )(in_vmem(half))
    got = swap(turned, "dom", over_xcore)

    def final_body(*refs):
        final_kernel(factor, *refs)

    grad_feats, grad_weight, grad_bias = call(
        final_body,
        [sds((ROWS, slots), F32), sds((2, ROWS, H), F32), sds((2, W), F32)],
        [SMEM, SMEM, VMEM, VMEM],
        [pltpu.VMEM((NB + 1, ROWS, W), F32)] * WAYS,
        nbytes=2**20,
        name="final",
    )(part_len, places, in_vmem(local_back), in_vmem(got))
    return (hidden, grad_feats, grad_weight, grad_bias.reshape(H))


def solution(mesh):
    placed = (
        P("col", "dom"),
        P("dom"),
        P("dom", None, None),
        P("dom", None),
        P("dom", None),
        P("dom", None),
        P("dom", None, None),
        P("dom", None),
        P(),
        P(),
        P(None, ("dom", "col")),
    )
    return jax.shard_map(
        shards,
        mesh=mesh,
        in_specs=placed,
        out_specs=(P(None, ("dom", "col")), P("col", "dom"), P(None, "col", None), P()),
        check_vma=False,
    )
```
